256 devices in a mesh: frame: 4 (over y), space: 64 (over x, z, core).
Axes of the slice: x: 4, y: 4, z: 8, core: 2. Of those that a mesh axis runs over, the one named last changes fastest.
Arguments:
- labels: int32 [128, 128, 512], P('space'), may hold values from 0 to 7
- region_conductivity: float32 [8], replicated, may hold values from 0.3 to 3
- source: float32 [4, 3, 64, 64, 256], P('frame', None, 'space'), may hold values from -9 to 9
- receivers: int32 [4, 3, 256], P('frame'), may hold values from 0 to 511, as said below
- observed: float32 [4, 256], P('frame'), may hold values from -2 to 2
Outputs:
- search_direction: float32 [4, 3, 64, 64, 256], P('frame', None, 'space')
- data_residual: float32 [4, 256], P('frame')
The draws below stay inside these ranges and needn't reach their ends.
Inputs may be any that keep to these rules, and one draw needn't show every extreme that they name: receivers[f, 0, k] is below 128, receivers[f, 1, k] below 128, receivers[f, 2, k] below 512.
All inputs are finite; a program needn't handle non-finite values.
Results may differ from the reference program's by a relative error of at most 0.0003.
Values sent between devices are 32-bit elements; how exact they have to be, the bound alone decides.
A program may use at most 64 MiB of HBM per device.

```python
import math
import jax
import jax.numpy as jnp
from jax import lax

NX = 128
NY = 512
RECV = 256
REGIONS = 8
ITERS = 3
NZ = 128
FRAMES = 4
NZC = 64
NXC = 64
NYC = 256
CELLS = 8388608


def draw_source(key, part):
    key = jax.random.fold_in(key, 5)
    depth = jnp.arange(NZC, dtype=jnp.float32)
    rising = (1.0 + 2.0 * depth / max(NZC - 1, 1))[:, None, None]
    array_shape = (FRAMES, 3, NZC, NXC, NYC)
    base = jnp.clip(jax.random.normal(key, array_shape, jnp.float32), -3.0, 3.0)
    return base * rising


def draw_receivers(key, part):
    key = jax.random.fold_in(key, 7)
    key_z, key_x, key_y = jax.random.split(key, 3)
    cell_z = jax.random.randint(key_z, (FRAMES, RECV), 0, NZ, jnp.int32)
    cell_x = jax.random.randint(key_x, (FRAMES, RECV), 0, NX, jnp.int32)
    cell_y = jax.random.randint(key_y, (FRAMES, RECV), 0, NY, jnp.int32)
    cell_z = cell_z.at[:, 0].set(NZ - 1).at[:, 1].set(0)
    cell_z = cell_z.at[:, 2].set(NZ // 2).at[:, 3].set(NZ // 2 - 1)
    cell_x = cell_x.at[:, 0].set(NX - 1)
    cell_y = cell_y.at[:, 0].set(NY - 1)
    return jnp.stack([cell_z, cell_x, cell_y], axis=1).astype(jnp.int32)


def set_ends(array, stream_key, smallest, top_value):
    dims = array.shape
    index_at = [jax.random.randint(jax.random.fold_in(stream_key, axis), (), 0, dims[axis]) for axis in range(len(dims))]
    array = array.at[tuple(index_at)].set(smallest)
    longest = dims.index(max(dims))
    index_at[longest] = (index_at[longest] + 1) % dims[longest]
    return array.at[tuple(index_at)].set(top_value)


def block_scale(own_key, dims, pieces, smallest, high):
    level = 1.0
    for dim, shards_of in pieces:
        draws = jax.random.uniform(jax.random.fold_in(jax.random.fold_in(own_key, 6), dim), (shards_of,), jnp.float32, smallest / len(pieces), high / len(pieces))
        level = level * jnp.repeat(jnp.exp(draws), dims[dim] // shards_of).reshape((-1,) + (1,) * (len(dims) - 1 - dim))
    return level


def centred(stream_key, extent, width, reach, shards=(), kind=jnp.bfloat16):
    entries = jax.random.normal(stream_key, extent, jnp.float32) * width
    if len(shards) > 0:
        entries = block_scale(stream_key, extent, shards, -0.22, 0.18) * entries
    return jnp.clip(entries, min=-reach, max=reach).astype(kind)


def setup_inputs(seed: int = 0) -> dict:
    key_of = jax.random.split(jax.random.key(seed), 6)
    labels = set_ends(jax.random.randint(key_of[0], (NZ, NX, NY), 0, REGIONS), jax.random.fold_in(key_of[0], 1), 0, REGIONS - 1).astype(jnp.int32)
    region_conductivity = jnp.clip(jnp.exp(jax.random.uniform(key_of[1], (REGIONS,), jnp.float32, math.log(0.3), math.log(3.0))), 0.3, 3.0)
    source = draw_source(jax.random.fold_in(key_of[5], 71), 0)
    receivers = draw_receivers(jax.random.fold_in(key_of[5], 71), 0)
    observed = centred(key_of[4], (FRAMES, RECV), 0.3, 2.0, ((0, 4),), jnp.float32)
    return {"labels": labels, "region_conductivity": region_conductivity, "source": source, "receivers": receivers, "observed": observed}


smoothing = 4.0


def conductivity(labels, region_conductivity):
    sigma_out = jnp.zeros(labels.shape, jnp.float32)
    for region in range(REGIONS):
        sigma_out = sigma_out + jnp.where(labels == region, region_conductivity[region], jnp.zeros((), jnp.float32))
    return sigma_out


def shifted_views(padded):
    return [padded[..., 2:, 1:-1, 1:-1], padded[..., :-2, 1:-1, 1:-1],
            padded[..., 1:-1, 2:, 1:-1], padded[..., 1:-1, :-2, 1:-1],
            padded[..., 1:-1, 1:-1, 2:], padded[..., 1:-1, 1:-1, :-2]]


def apply_operator(values, sigma_pad, values_pad):
    center = sigma_pad[1:-1, 1:-1, 1:-1]
    result = jnp.zeros_like(values)
    for sigma_near, values_near in zip(shifted_views(sigma_pad), shifted_views(values_pad)):
        result = result + 0.5 * (center + sigma_near) * (values - values_near)
    return result


def previous_along(values, axis_pos):
    pad_width = [(0, 0)] * values.ndim
    pad_width[axis_pos] = (1, 0)
    return lax.slice_in_dim(jnp.pad(values, pad_width), 0, values.shape[axis_pos], axis=axis_pos)


def following_along(values, axis_pos):
    pad_width = [(0, 0)] * values.ndim
    pad_width[axis_pos] = (0, 1)
    return lax.slice_in_dim(jnp.pad(values, pad_width), 1, values.shape[axis_pos] + 1, axis=axis_pos)


def prolong(coarse):
    return jnp.repeat(jnp.repeat(jnp.repeat(coarse, 2, axis=-3), 2, axis=-2), 2, axis=-1)


def restrict(fine):
    shape_in = fine.shape
    blocks = fine.reshape(shape_in[:-3] + (shape_in[-3] // 2, 2, shape_in[-2] // 2, 2, shape_in[-1] // 2, 2))
    return jnp.sum(blocks, axis=(-5, -3, -1))


def chain_tables(count):
    def stepper(before, frame_pos):
        neighbours = (frame_pos > 0).astype(jnp.float32) + (frame_pos < count - 1).astype(jnp.float32)
        diagonal = 1.0 + smoothing * neighbours
        coupled = jnp.where(frame_pos > 0, smoothing * smoothing / before, jnp.zeros((), jnp.float32))
        denom = diagonal - coupled
        return denom, denom

    _, dens = lax.scan(stepper, jnp.ones((), jnp.float32), jnp.arange(count, dtype=jnp.int32))
    return dens, smoothing / dens


def smooth_frames(gradient, dens, rates):
    def forward_step(carry, item_parts):
        grad_now, denom, rate = item_parts
        nxt = grad_now / denom + rate * carry
        return nxt, nxt

    def backward_step(carry, item_parts):
        dvals, rate = item_parts
        nxt = dvals + rate * carry
        return nxt, nxt

    start_state = jnp.zeros(gradient.shape[1:], jnp.float32)
    _, dprime = lax.scan(forward_step, start_state, (gradient, dens, rates))
    _, solved = lax.scan(backward_step, start_state, (dprime, rates), reverse=True)
    return solved


def solve_cg(rhs, sigma_pad):
    def operate(values):
        return apply_operator(values, sigma_pad, jnp.pad(values, 1))

    solution = jnp.zeros_like(rhs)
    residual = rhs
    direction = rhs
    norm_now = jnp.sum(residual * residual)
    for iteration in range(ITERS):
        image = operate(direction)
        alpha = norm_now / jnp.sum(direction * image)
        solution = solution + alpha * direction
        residual = residual - alpha * image
        norm_next = jnp.sum(residual * residual)
        direction = residual + (norm_next / norm_now) * direction
        norm_now = norm_next
    return solution


def divergence(frame_source):
    total = jnp.zeros(frame_source.shape[1:], jnp.float32)
    for comp in range(3):
        total = total + frame_source[comp] - previous_along(frame_source[comp], comp)
    return total


def adjoint_divergence(coarse):
    return jnp.stack([coarse - following_along(coarse, comp) for comp in range(3)], axis=0)


def reference(labels, region_conductivity, source, receivers, observed):
    sigma_pad = jnp.pad(conductivity(labels, region_conductivity), 1)

    def one_frame(frame_item):
        frame_source, frame_receivers, frame_observed = frame_item
        flat_cell = ((frame_receivers[0] * NX + frame_receivers[1]) * NY + frame_receivers[2]).astype(jnp.int32)
        rhs = prolong(divergence(frame_source))
        potential = solve_cg(rhs, sigma_pad)
        misfit = potential.reshape(-1)[flat_cell] - frame_observed
        adjoint_rhs = jnp.zeros((CELLS,), jnp.float32).at[flat_cell].add(misfit).reshape(NZ, NX, NY)
        adjoint = solve_cg(adjoint_rhs, sigma_pad)
        return adjoint_divergence(restrict(adjoint)), misfit

    gradient, data_residual = lax.map(one_frame, (source, receivers, observed))
    dens, rates = chain_tables(FRAMES)
    return smooth_frames(gradient, dens, rates), data_residual
```

```python
import functools

import jax
import jax.numpy as jnp
import numpy as np
from jax import lax
from jax.experimental import pallas as pl
from jax.experimental.pallas import tpu as pltpu
from jax.sharding import PartitionSpec as P

SMOOTHING = 4.0
PAD = 8
ROWS = 8
PLANES = 7
MESH = pl.DeviceIdType.MESH
F32 = jnp.float32
BF16 = jnp.bfloat16


def smoothing_inverse(frames):
    matrix = np.zeros((frames, frames))
    for f in range(frames):
        near = [g for g in (f - 1, f + 1) if 0 <= g < frames]
        matrix[f, f] = 1.0 + SMOOTHING * len(near)
        for g in near:
            matrix[f, g] = -SMOOTHING
    return np.linalg.inv(matrix)


def parts_of(x):
    high = x.astype(BF16)
    rest = x - high.astype(F32)
    middle = rest.astype(BF16)
    low = (rest - middle.astype(F32)).astype(BF16)
    return high, middle, low


def dot(a, b):
    return jnp.dot(a, b, preferred_element_type=F32)


def lanes_to_sublanes(row):
    n = row.shape[1]
    same = lax.broadcasted_iota(jnp.int32, (n, n), 0) == lax.broadcasted_iota(jnp.int32, (n, n), 1)
    return jnp.sum(jnp.where(same, row, jnp.zeros_like(row)), axis=1, keepdims=True)


def sublanes_to_lanes(column):
    n = column.shape[0]
    same = lax.broadcasted_iota(jnp.int32, (n, n), 0) == lax.broadcasted_iota(jnp.int32, (n, n), 1)
    return jnp.sum(jnp.where(same, column, jnp.zeros_like(column)), axis=0, keepdims=True)


def folded(x):
    total = x[:, :128]
    for start in range(128, x.shape[1], 128):
        total = total + x[:, start : start + 128]
    return total


def cg_coefficients(m):
    m0, m1, m2, m3, m4, m5 = m
    a0 = m0 / m1
    rr1 = m0 - 2.0 * a0 * m1 + a0 * a0 * m2
    b0 = rr1 / m0
    p0, p1 = 1.0 + b0, -a0
    a1 = rr1 / (p0 * p0 * m1 + 2.0 * p0 * p1 * m2 + p1 * p1 * m3)
    r0, r1, r2 = 1.0, -a0 - a1 * p0, -a1 * p1
    rr2 = m0 + r1 * r1 * m2 + r2 * r2 * m4 + 2.0 * (r1 * m1 + r2 * m2 + r1 * r2 * m3)
    b1 = rr2 / rr1
    q0, q1, q2 = r0 + b1 * p0, r1 + b1 * p1, r2
    curv = q0 * q0 * m1 + q1 * q1 * m3 + q2 * q2 * m5
    curv = curv + 2.0 * (q0 * q1 * m2 + q0 * q2 * m3 + q1 * q2 * m4)
    a2 = rr2 / curv
    return a0 + a1 * p0 + a2 * q0, a1 * p1 + a2 * q1, a2 * q2


def kernel(
    frames, slabs, regions,
    labels_ref, cond_ref, source_ref, recv_ref, obs_ref,
    out_ref, misfit_ref,
    lab, src, h, v0, v1, v2, diag, kxo, kxm, kyo, kym, kz,
    czb, qs, up, tall, gat, hot_y, msg, got1, got2, pmsg, pgot, dmsg, dgot, wc, wg, uq, uf,
    load_sem, h_send, h_recv, q_send, q_recv, ar_send, ar_recv, p_send, p_recv, y_send, y_recv,
):
    nx, ny = lab.shape[1], lab.shape[2]
    nxc, nyc = nx // 2, ny // 2
    recv = recv_ref.shape[1]
    quarter = nxc // frames
    chunks = nx // ROWS
    f = lax.axis_index("frame")
    s = lax.axis_index("space")

    def slab_at(by):
        return lax.rem(s + by + slabs, slabs)

    def frame_at(by):
        return lax.rem(f + by, frames)

    barrier = pltpu.get_barrier_semaphore()

    def greet(k, carry):
        pl.semaphore_signal(barrier, inc=1, device_id=(f, slab_at(k)), device_id_type=MESH)
        return carry

    lax.fori_loop(1, slabs, greet, 0)
    for k in range(1, frames):
        for by in (0, 1, -1):
            pl.semaphore_signal(barrier, inc=1, device_id=(frame_at(k), slab_at(by)), device_id_type=MESH)
    greeted = slabs - 1 + 3 * (frames - 1)

    load_labels = pltpu.make_async_copy(labels_ref, lab, load_sem.at[0])
    load_source = pltpu.make_async_copy(source_ref, src, load_sem.at[1])
    load_labels.start()
    load_source.start()

    zero_rows = jnp.zeros((PAD, ny), F32)
    for field in (h, v0, v1, v2):
        for p in range(PLANES):
            field[p, 0:PAD, :] = zero_rows
            field[p, PAD + nx : PAD + nx + PAD, :] = zero_rows
    first = 2 * s - 2
    zx_row = (recv_ref[0:1, :] - first) * nx + recv_ref[1:2, :]
    zx_col = lanes_to_sublanes(zx_row)
    y_col = lanes_to_sublanes(recv_ref[2:3, :])
    own_ids = lax.broadcasted_iota(jnp.int32, (recv, 2 * nx), 1) + 2 * nx
    gat[...] = (zx_col == own_ids).astype(BF16)
    hot_y[...] = (y_col == lax.broadcasted_iota(jnp.int32, (recv, ny), 1)).astype(BF16)
    coarse_id = lax.broadcasted_iota(jnp.int32, (nyc, ny), 0)
    up[...] = (coarse_id == lax.broadcasted_iota(jnp.int32, (nyc, ny), 1) // 2).astype(BF16)
    z_in = recv_ref[0:1, :] - 2 * s
    inside = (z_in >= 0) & (z_in < 2)

    load_labels.wait()

    def convert(i, carry):
        p, r = i // chunks, i % chunks
        here = lab[p, pl.ds(pl.multiple_of(r * ROWS, ROWS), ROWS), :]
        value = jnp.full((ROWS, ny), 0.5 * cond_ref[0], F32)
        for region in range(1, regions):
            value = jnp.where(here == region, 0.5 * cond_ref[region], value)
        h[p + 2, pl.ds(pl.multiple_of(PAD + r * ROWS, ROWS), ROWS), :] = value
        return carry

    lax.fori_loop(0, 2 * chunks, convert, 0)
    load_source.wait()

    pl.semaphore_wait(barrier, greeted)

    def send(src_ref, dst_ref, sems, index, device):
        copy = pltpu.make_async_remote_copy(
            src_ref=src_ref, dst_ref=dst_ref, send_sem=sems[0].at[index], recv_sem=sems[1].at[index],
            device_id=device, device_id_type=MESH,
        )
        copy.start()
        return copy

    def plane(p):
        return h.at[p, pl.ds(PAD, nx), :]

    copy_cz = send(src.at[0], czb, (q_send, q_recv), 0, (f, slab_at(1)))
    h_sems = (h_send, h_recv)
    copy_h1 = send(plane(3), plane(1), h_sems, 0, (f, slab_at(1)))
    copy_h4 = send(plane(2), plane(4), h_sems, 1, (f, slab_at(-1)))
    copy_h0 = send(plane(2), plane(0), h_sems, 2, (f, slab_at(1)))
    copy_h5 = send(plane(3), plane(5), h_sems, 3, (f, slab_at(-1)))
    copy_h6 = send(plane(2), plane(6), h_sems, 4, (f, slab_at(-2)))

    row_c = lax.broadcasted_iota(jnp.int32, (nxc, nyc), 0)
    lane_c = lax.broadcasted_iota(jnp.int32, (nxc, nyc), 1)
    along_x, along_y = src[1], src[2]
    total = src[0] + along_x - jnp.where(row_c > 0, pltpu.roll(along_x, 1, 0), 0.0)
    total = total + along_y - jnp.where(lane_c > 0, pltpu.roll(along_y, 1, 1), 0.0)
    copy_cz.wait_recv()
    qs[1] = total - jnp.where(s > 0, czb[...], 0.0)
    q_sems = (q_send, q_recv)
    copies_q = [
        send(qs.at[1], qs.at[0], q_sems, 1, (f, slab_at(1))),
        send(qs.at[1], qs.at[2], q_sems, 2, (f, slab_at(-1))),
        send(qs.at[1], qs.at[3], q_sems, 3, (f, slab_at(-2))),
    ]

    def valid(p):
        z = first + p
        return (z >= 0) & (z < 2 * slabs)

    def aligned(r):
        return pl.ds(pl.multiple_of(PAD + r * ROWS, ROWS), ROWS)

    def next_row(field, p, r, here):
        return pltpu.roll(jnp.where(sub == 0, field[p, aligned(r + 1), :], here), ROWS - 1, 0)

    def previous_row(field, p, r, here):
        return pltpu.roll(jnp.where(sub == ROWS - 1, field[p, aligned(r - 1), :], here), 1, 0)

    def prolong(c):
        z = s - 1 + c
        ok = (z >= 0) & (z < slabs)
        high, middle, low = parts_of(jnp.where(ok, qs[c], 0.0))
        fine = dot(high, up[...]) + dot(middle, up[...]) + dot(low, up[...])
        for t in range(ny // 128):
            tall[t, pl.ds(0, nxc, 2), :] = fine[:, t * 128 : t * 128 + 128]
            tall[t, pl.ds(1, nxc, 2), :] = fine[:, t * 128 : t * 128 + 128]
        for p in (2 * c, 2 * c + 1):
            if p < PLANES:
                for t in range(ny // 128):
                    v0[p, PAD : PAD + nx, t * 128 : t * 128 + 128] = tall[t]

    lane = lax.broadcasted_iota(jnp.int32, (ROWS, ny), 1)
    sub = lax.broadcasted_iota(jnp.int32, (ROWS, ny), 0)

    def zero_outside(p):
        @pl.when(jnp.logical_not(valid(p)))
        def _():
            h[p, PAD : PAD + nx, :] = jnp.zeros((nx, ny), F32)

    def vertical(e):
        keep = jnp.where(valid(e) & valid(e + 1), 1.0, 0.0).astype(F32)

        def body(r, carry):
            kz[e, pl.ds(pl.multiple_of(r * ROWS, ROWS), ROWS), :] = keep * (h[e, aligned(r), :] + h[e + 1, aligned(r), :])
            return carry

        lax.fori_loop(0, chunks, body, 0)

    def coefficients(p):
        def body(r, carry):
            at = pl.ds(pl.multiple_of(r * ROWS, ROWS), ROWS)
            here = h[p, aligned(r), :]
            x_next, x_prev = next_row(h, p, r, here), previous_row(h, p, r, here)
            y_next = jnp.where(lane < ny - 1, pltpu.roll(here, ny - 1, 1), 0.0)
            y_prev = jnp.where(lane > 0, pltpu.roll(here, 1, 1), 0.0)
            kxo[p, at, :] = here + x_next
            kxm[p, at, :] = here + x_prev
            kyo[p, at, :] = jnp.where(lane < ny - 1, here + y_next, 0.0)
            kym[p, at, :] = jnp.where(lane > 0, here + y_prev, 0.0)
            near = x_next + x_prev + y_next + y_prev
            diag[p, at, :] = 6.0 * here + near + h[p - 1, aligned(r), :] + h[p + 1, aligned(r), :]
            return carry

        lax.fori_loop(0, chunks, body, 0)

    def operate(src_v, dst_v, p, with_moments, sums):
        def body(r, carry):
            at = pl.ds(pl.multiple_of(r * ROWS, ROWS), ROWS)
            here = src_v[p, aligned(r), :]
            value = diag[p, at, :] * here
            value = value - kxo[p, at, :] * next_row(src_v, p, r, here)
            value = value - kxm[p, at, :] * previous_row(src_v, p, r, here)
            value = value - kyo[p, at, :] * pltpu.roll(here, ny - 1, 1)
            value = value - kym[p, at, :] * pltpu.roll(here, 1, 1)
            value = value - kz[p, at, :] * src_v[p + 1, aligned(r), :]
            value = value - kz[p - 1, at, :] * src_v[p - 1, aligned(r), :]
            dst_v[p, aligned(r), :] = value
            if not with_moments:
                return carry
            return (carry[0] + folded(here * value), carry[1] + folded(value * value))

        return lax.fori_loop(0, chunks, body, sums)

    def square(src_v, p, total):
        def body(r, carry):
            here = src_v[p, aligned(r), :]
            return carry + folded(here * here)

        return lax.fori_loop(0, chunks, body, total)

    def energy(field, p, total):
        def body(r, carry):
            at = pl.ds(pl.multiple_of(r * ROWS, ROWS), ROWS)
            here = field[p, aligned(r), :]
            near = kxo[p, at, :] * next_row(field, p, r, here)
            near = near + kyo[p, at, :] * pltpu.roll(here, ny - 1, 1)
            near = near + kz[p, at, :] * field[p + 1, aligned(r), :]
            return carry + folded(here * (diag[p, at, :] * here - 2.0 * near))

        return lax.fori_loop(0, chunks, body, total)

    nothing = jnp.zeros((ROWS, 128), F32)

    def krylov_own():
        m0 = square(v0, 3, square(v0, 2, nothing))
        return m0, operate(v0, v1, 3, True, operate(v0, v1, 2, True, (nothing, nothing)))

    def krylov_rest(m0, m12):
        for p in (1, 4, 5):
            operate(v0, v1, p, False, 0)
        m34 = operate(v1, v2, 3, True, operate(v1, v2, 2, True, (nothing, nothing)))
        operate(v1, v2, 4, False, 0)
        m5 = energy(v2, 3, energy(v2, 2, nothing))
        sums = [jnp.sum(jnp.sum(m, axis=0, keepdims=True), axis=1, keepdims=True) for m in (m0, *m12, *m34, m5)]
        place = lax.broadcasted_iota(jnp.int32, (1, 128), 1)
        row = jnp.zeros((1, 128), F32)
        for j, m in enumerate(sums):
            row = jnp.where(place == j, m, row)
        return row

    def share(source, landing, index):
        def start(k, carry):
            pltpu.make_async_remote_copy(
                src_ref=source, dst_ref=landing.at[s], send_sem=ar_send.at[index], recv_sem=ar_recv.at[index],
                device_id=(f, slab_at(k)), device_id_type=MESH,
            ).start()
            return carry

        lax.fori_loop(1, slabs, start, 0)

    def shared(landing, index):
        others = landing.at[pl.ds(0, slabs - 1)]
        whole = pltpu.make_async_remote_copy(
            src_ref=others, dst_ref=others, send_sem=ar_send.at[index], recv_sem=ar_recv.at[index],
            device_id=(f, slab_at(1)), device_id_type=MESH,
        )
        whole.wait_send()
        whole.wait_recv()

    def moments_of(landing):
        total = jnp.sum(landing[...], axis=0)
        return [total[:, j : j + 1] for j in range(6)]

    copy_h1.wait_recv()
    copy_h4.wait_recv()
    zero_outside(1)
    zero_outside(4)
    for e in (1, 2, 3):
        vertical(e)
    for p in (2, 3):
        coefficients(p)
    for copy in copies_q:
        copy.wait_recv()
    for c in range(4):
        prolong(c)
    m0, m12 = krylov_own()
    copy_h0.wait_recv()
    copy_h5.wait_recv()
    copy_h6.wait_recv()
    for p in (0, 5, 6):
        zero_outside(p)
    for e in (0, 4, 5):
        vertical(e)
    for p in (1, 4, 5):
        coefficients(p)
    moments = krylov_rest(m0, m12)
    msg[0] = moments
    got1[s] = moments
    share(msg.at[0], got1, 0)

    for j, field in enumerate((v0, v1, v2)):
        whole = jnp.concatenate([field[2, PAD : PAD + nx, :], field[3, PAD : PAD + nx, :]], axis=0)
        rows = sum(dot(gat[...], part) for part in parts_of(whole))
        column = jnp.sum(rows * hot_y[...].astype(F32), axis=1, keepdims=True)
        pmsg[j] = sublanes_to_lanes(column)
    p_sems = (p_send, p_recv)
    copies_p = [
        send(pmsg, pgot.at[0], p_sems, 0, (f, slab_at(1))),
        send(pmsg, pgot.at[1], p_sems, 1, (f, slab_at(-1))),
        send(pmsg, pgot.at[2], p_sems, 2, (f, slab_at(-2))),
    ]
    shared(got1, 0)
    c0, c1, c2 = cg_coefficients(moments_of(got1))
    observed = obs_ref[...]

    def misfit(values):
        return c0 * values[0] + c1 * values[1] + c2 * values[2] - observed

    mine = jnp.where(inside, misfit([pmsg[j] for j in range(3)]), 0.0)
    dmsg[...] = mine
    dgot[s] = mine
    share(dmsg, dgot, 1)
    for copy in copies_p:
        copy.wait_recv()
    d = misfit([pmsg[j] + pgot[0, j] + pgot[1, j] + pgot[2, j] for j in range(3)])

    d_parts = parts_of(d)
    for p in range(PLANES):
        hit = zx_row == lax.broadcasted_iota(jnp.int32, (nx, recv), 0) + p * nx
        value = sum(dot(jnp.where(hit, part.astype(F32), 0.0).astype(BF16), hot_y[...]) for part in d_parts)
        v0[p, PAD : PAD + nx, :] = jnp.where(valid(p), value, 0.0)
    moments = krylov_rest(*krylov_own())
    msg[1] = moments
    got2[s] = moments
    share(msg.at[1], got2, 2)
    shared(got2, 2)
    c0, c1, c2 = cg_coefficients(moments_of(got2))

    def restrict(r, carry):
        at = aligned(r)
        fine = [c0 * v0[p, at, :] + c1 * v1[p, at, :] + c2 * v2[p, at, :] for p in (2, 3)]
        both = fine[0] + fine[1]
        for t in range(ny // 128):
            tall[t, pl.ds(pl.multiple_of(r * ROWS, ROWS), ROWS), :] = both[:, t * 128 : t * 128 + 128]
        return carry

    lax.fori_loop(0, chunks, restrict, 0)
    pairs = jnp.concatenate(
        [tall[t, pl.ds(0, nxc, 2), :] + tall[t, pl.ds(1, nxc, 2), :] for t in range(ny // 128)], axis=1
    )
    down = (((1,), (1,)), ((), ()))
    wc[...] = sum(lax.dot_general(part, up[...], down, preferred_element_type=F32) for part in parts_of(pairs))

    def part_at(g):
        return pl.ds(pl.multiple_of(g * quarter, quarter), quarter)

    wg[f] = wc[part_at(f), :]
    y_sems = (y_send, y_recv)
    copies_w = [
        send(wc.at[part_at(frame_at(k)), :], wg.at[f], y_sems, k - 1, (frame_at(k), s)) for k in range(1, frames)
    ]
    for copy in copies_w:
        copy.wait_recv()
    inverse = smoothing_inverse(frames)
    for g in range(frames):
        uq[g] = sum(float(inverse[g, k]) * wg[k] for k in range(frames))
    uf[0, part_at(f), :] = uq[f]
    copies_u = []
    for k in range(frames):
        to = frame_at(k)
        copies_u.append(send(uq.at[to], uf.at[1, part_at(f), :], y_sems, 2 * frames + k, (to, slab_at(-1))))
        if k > 0:
            copies_u.append(send(uq.at[to], uf.at[0, part_at(f), :], y_sems, frames + k, (to, s)))
    shared(dgot, 1)
    misfit_ref[...] = jnp.sum(dgot[...], axis=0)
    for copy in copies_u:
        copy.wait_recv()
    u = uf[0]
    out_ref[0] = u - jnp.where(s < slabs - 1, uf[1], 0.0)
    out_ref[1] = u - jnp.where(row_c < nxc - 1, pltpu.roll(u, nxc - 1, 0), 0.0)
    out_ref[2] = u - jnp.where(lane_c < nyc - 1, pltpu.roll(u, nyc - 1, 1), 0.0)
    for copy in [copy_cz, copy_h0, copy_h1, copy_h4, copy_h5, copy_h6, *copies_q, *copies_p, *copies_w, *copies_u]:
        copy.wait_send()


def shards(frames, slabs, labels, region_conductivity, source, receivers, observed):
    _, nx, ny = labels.shape
    nxc, nyc = nx // 2, ny // 2
    recv = receivers.shape[2]
    quarter = nxc // frames
    vmem = pl.BlockSpec(memory_space=pltpu.VMEM)
    plane = (PLANES, nx, ny)
    padded = (PLANES, nx + 2 * PAD, ny)
    scratch = [
        pltpu.VMEM((2, nx, ny), jnp.int32),
        pltpu.VMEM((3, nxc, nyc), F32),
        *[pltpu.VMEM(padded, F32) for _ in range(4)],
        *[pltpu.VMEM(plane, F32) for _ in range(6)],
        pltpu.VMEM((nxc, nyc), F32),
        pltpu.VMEM((4, nxc, nyc), F32),
        pltpu.VMEM((nyc, ny), BF16),
        pltpu.VMEM((ny // 128, nx, 128), F32),
        pltpu.VMEM((recv, 2 * nx), BF16),
        pltpu.VMEM((recv, ny), BF16),
        pltpu.VMEM((2, 1, 128), F32),
        pltpu.VMEM((slabs, 1, 128), F32),
        pltpu.VMEM((slabs, 1, 128), F32),
        pltpu.VMEM((3, 1, recv), F32),
        pltpu.VMEM((3, 3, 1, recv), F32),
        pltpu.VMEM((1, recv), F32),
        pltpu.VMEM((slabs, 1, recv), F32),
        pltpu.VMEM((nxc, nyc), F32),
        pltpu.VMEM((frames, quarter, nyc), F32),
        pltpu.VMEM((frames, quarter, nyc), F32),
        pltpu.VMEM((2, nxc, nyc), F32),
        pltpu.SemaphoreType.DMA((2,)),
        *[pltpu.SemaphoreType.DMA((5,)) for _ in range(2)],
        *[pltpu.SemaphoreType.DMA((4,)) for _ in range(2)],
        *[pltpu.SemaphoreType.DMA((3,)) for _ in range(2)],
        *[pltpu.SemaphoreType.DMA((3,)) for _ in range(2)],
        *[pltpu.SemaphoreType.DMA((3 * frames,)) for _ in range(2)],
    ]
    out, misfit = pl.pallas_call(
        functools.partial(kernel, frames, slabs, region_conductivity.shape[0]),
        out_shape=(jax.ShapeDtypeStruct((3, nxc, nyc), F32), jax.ShapeDtypeStruct((1, recv), F32)),
        in_specs=[
            pl.BlockSpec(memory_space=pl.ANY),
            pl.BlockSpec(memory_space=pltpu.SMEM),
            pl.BlockSpec(memory_space=pl.ANY),
            vmem,
            vmem,
        ],
        out_specs=(vmem, vmem),
        scratch_shapes=scratch,
        compiler_params=pltpu.CompilerParams(
            collective_id=0, has_side_effects=True, vmem_limit_bytes=48 * 1024 * 1024
        ),
    )(labels, region_conductivity, source.reshape(3, nxc, nyc), receivers[0], observed)
    return out.reshape(1, 3, 1, nxc, nyc), misfit


def solution(mesh):
    in_specs = (
        P("space", None, None),
        P(),
        P("frame", None, "space", None, None),
        P("frame", None, None),
        P("frame", None),
    )
    out_specs = (P("frame", None, "space", None, None), P("frame", None))
    body = functools.partial(shards, mesh.shape["frame"], mesh.shape["space"])
    return jax.shard_map(body, mesh=mesh, in_specs=in_specs, out_specs=out_specs, check_vma=False)
```

```python
import functools

import jax
import jax.numpy as jnp
import numpy as np
from jax import lax
from jax.experimental import pallas as pl
from jax.experimental.pallas import tpu as pltpu
from jax.sharding import PartitionSpec as P

SMOOTHING = 4.0
PAD = 8
ROWS = 8
PLANES = 7
MESH = pl.DeviceIdType.MESH
F32 = jnp.float32
BF16 = jnp.bfloat16


def smoothing_inverse(frames):
    matrix = np.zeros((frames, frames))
    for f in range(frames):
        near = [g for g in (f - 1, f + 1) if 0 <= g < frames]
        matrix[f, f] = 1.0 + SMOOTHING * len(near)
        for g in near:
            matrix[f, g] = -SMOOTHING
    return np.linalg.inv(matrix)


def parts_of(x):
    high = x.astype(BF16)
    rest = x - high.astype(F32)
    middle = rest.astype(BF16)
    low = (rest - middle.astype(F32)).astype(BF16)
    return high, middle, low


def dot(a, b):
    return jnp.dot(a, b, preferred_element_type=F32)


def lanes_to_sublanes(row):
    n = row.shape[1]
    same = lax.broadcasted_iota(jnp.int32, (n, n), 0) == lax.broadcasted_iota(jnp.int32, (n, n), 1)
    return jnp.sum(jnp.where(same, row, jnp.zeros_like(row)), axis=1, keepdims=True)


def sublanes_to_lanes(column):
    n = column.shape[0]
    same = lax.broadcasted_iota(jnp.int32, (n, n), 0) == lax.broadcasted_iota(jnp.int32, (n, n), 1)
    return jnp.sum(jnp.where(same, column, jnp.zeros_like(column)), axis=0, keepdims=True)


def folded(x):
    total = x[:, :128]
    for start in range(128, x.shape[1], 128):
        total = total + x[:, start : start + 128]
    return total


def cg_coefficients(m):
    m0, m1, m2, m3, m4, m5 = m
    a0 = m0 / m1
    rr1 = m0 - 2.0 * a0 * m1 + a0 * a0 * m2
    b0 = rr1 / m0
    p0, p1 = 1.0 + b0, -a0
    a1 = rr1 / (p0 * p0 * m1 + 2.0 * p0 * p1 * m2 + p1 * p1 * m3)
    r0, r1, r2 = 1.0, -a0 - a1 * p0, -a1 * p1
    rr2 = m0 + r1 * r1 * m2 + r2 * r2 * m4 + 2.0 * (r1 * m1 + r2 * m2 + r1 * r2 * m3)
    b1 = rr2 / rr1
    q0, q1, q2 = r0 + b1 * p0, r1 + b1 * p1, r2
    curv = q0 * q0 * m1 + q1 * q1 * m3 + q2 * q2 * m5
    curv = curv + 2.0 * (q0 * q1 * m2 + q0 * q2 * m3 + q1 * q2 * m4)
    a2 = rr2 / curv
    return a0 + a1 * p0 + a2 * q0, a1 * p1 + a2 * q1, a2 * q2


def kernel(
    frames, slabs, regions,
    labels_ref, cond_ref, source_ref, recv_ref, obs_ref,
    out_ref, misfit_ref,
    lab, src, h, v0, v1, v2, diag, kxo, kxm, kyo, kym, kz,
    czb, qs, up, tall, gat, hot_y, msg, got1, got2, pmsg, pgot, dmsg, dgot, wc, wg, uq, uf,
    load_sem, h_send, h_recv, q_send, q_recv, ar_send, ar_recv, p_send, p_recv, y_send, y_recv,
):
    nx, ny = lab.shape[1], lab.shape[2]
    nxc, nyc = nx // 2, ny // 2
    recv = recv_ref.shape[1]
    quarter = nxc // frames
    chunks = nx // ROWS
    f = lax.axis_index("frame")
    s = lax.axis_index("space")

    def slab_at(by):
        return lax.rem(s + by + slabs, slabs)

    def frame_at(by):
        return lax.rem(f + by, frames)

    barrier = pltpu.get_barrier_semaphore()

    def greet(k, carry):
        pl.semaphore_signal(barrier, inc=1, device_id=(f, slab_at(k)), device_id_type=MESH)
        return carry

    lax.fori_loop(1, slabs, greet, 0)
    for k in range(1, frames):
        for by in (0, 1, -1):
            pl.semaphore_signal(barrier, inc=1, device_id=(frame_at(k), slab_at(by)), device_id_type=MESH)
    greeted = slabs - 1 + 3 * (frames - 1)

    load_labels = pltpu.make_async_copy(labels_ref, lab, load_sem.at[0])
    load_source = pltpu.make_async_copy(source_ref, src, load_sem.at[1])
    load_labels.start()
    load_source.start()

    zero_rows = jnp.zeros((PAD, ny), F32)
    for field in (h, v0, v1, v2):
        for p in range(PLANES):
            field[p, 0:PAD, :] = zero_rows
            field[p, PAD + nx : PAD + nx + PAD, :] = zero_rows
    first = 2 * s - 2
    zx_row = (recv_ref[0:1, :] - first) * nx + recv_ref[1:2, :]
    zx_col = lanes_to_sublanes(zx_row)
    y_col = lanes_to_sublanes(recv_ref[2:3, :])
    own_ids = lax.broadcasted_iota(jnp.int32, (recv, 2 * nx), 1) + 2 * nx
    gat[...] = (zx_col == own_ids).astype(BF16)
    hot_y[...] = (y_col == lax.broadcasted_iota(jnp.int32, (recv, ny), 1)).astype(BF16)
    coarse_id = lax.broadcasted_iota(jnp.int32, (nyc, ny), 0)
    up[...] = (coarse_id == lax.broadcasted_iota(jnp.int32, (nyc, ny), 1) // 2).astype(BF16)
    z_in = recv_ref[0:1, :] - 2 * s
    inside = (z_in >= 0) & (z_in < 2)

    load_labels.wait()

    def convert(i, carry):
        p, r = i // chunks, i % chunks
        here = lab[p, pl.ds(pl.multiple_of(r * ROWS, ROWS), ROWS), :]
        value = jnp.full((ROWS, ny), 0.5 * cond_ref[0], F32)
        for region in range(1, regions):
            value = jnp.where(here == region, 0.5 * cond_ref[region], value)
        h[p + 2, pl.ds(pl.multiple_of(PAD + r * ROWS, ROWS), ROWS), :] = value
        return carry

    lax.fori_loop(0, 2 * chunks, convert, 0, unroll=chunks)
    load_source.wait()

    pl.semaphore_wait(barrier, greeted)

    def send(src_ref, dst_ref, sems, index, device):
        copy = pltpu.make_async_remote_copy(
            src_ref=src_ref, dst_ref=dst_ref, send_sem=sems[0].at[index], recv_sem=sems[1].at[index],
            device_id=device, device_id_type=MESH,
        )
        copy.start()
        return copy

    def plane(p):
        return h.at[p, pl.ds(PAD, nx), :]

    copy_cz = send(src.at[0], czb, (q_send, q_recv), 0, (f, slab_at(1)))
    h_sems = (h_send, h_recv)
    copy_h1 = send(plane(3), plane(1), h_sems, 0, (f, slab_at(1)))
    copy_h4 = send(plane(2), plane(4), h_sems, 1, (f, slab_at(-1)))
    copy_h0 = send(plane(2), plane(0), h_sems, 2, (f, slab_at(1)))
    copy_h5 = send(plane(3), plane(5), h_sems, 3, (f, slab_at(-1)))
    copy_h6 = send(plane(2), plane(6), h_sems, 4, (f, slab_at(-2)))

    row_c = lax.broadcasted_iota(jnp.int32, (nxc, nyc), 0)
    lane_c = lax.broadcasted_iota(jnp.int32, (nxc, nyc), 1)
    along_x, along_y = src[1], src[2]
    total = src[0] + along_x - jnp.where(row_c > 0, pltpu.roll(along_x, 1, 0), 0.0)
    total = total + along_y - jnp.where(lane_c > 0, pltpu.roll(along_y, 1, 1), 0.0)
    copy_cz.wait_recv()
    qs[1] = total - jnp.where(s > 0, czb[...], 0.0)
    q_sems = (q_send, q_recv)
    copies_q = [
        send(qs.at[1], qs.at[0], q_sems, 1, (f, slab_at(1))),
        send(qs.at[1], qs.at[2], q_sems, 2, (f, slab_at(-1))),
        send(qs.at[1], qs.at[3], q_sems, 3, (f, slab_at(-2))),
    ]

    def valid(p):
        z = first + p
        return (z >= 0) & (z < 2 * slabs)

    def aligned(r):
        return pl.ds(pl.multiple_of(PAD + r * ROWS, ROWS), ROWS)

    def next_row(field, p, r, here):
        return pltpu.roll(jnp.where(sub == 0, field[p, aligned(r + 1), :], here), ROWS - 1, 0)

    def previous_row(field, p, r, here):
        return pltpu.roll(jnp.where(sub == ROWS - 1, field[p, aligned(r - 1), :], here), 1, 0)

    def prolong(c):
        z = s - 1 + c
        ok = (z >= 0) & (z < slabs)
        high, middle, low = parts_of(jnp.where(ok, qs[c], 0.0))
        fine = dot(high, up[...]) + dot(middle, up[...]) + dot(low, up[...])
        for t in range(ny // 128):
            tall[t, pl.ds(0, nxc, 2), :] = fine[:, t * 128 : t * 128 + 128]
            tall[t, pl.ds(1, nxc, 2), :] = fine[:, t * 128 : t * 128 + 128]
        for p in (2 * c, 2 * c + 1):
            if p < PLANES:
                for t in range(ny // 128):
                    v0[p, PAD : PAD + nx, t * 128 : t * 128 + 128] = tall[t]

    lane = lax.broadcasted_iota(jnp.int32, (ROWS, ny), 1)
    sub = lax.broadcasted_iota(jnp.int32, (ROWS, ny), 0)

    def zero_outside(p):
        @pl.when(jnp.logical_not(valid(p)))
        def _():
            h[p, PAD : PAD + nx, :] = jnp.zeros((nx, ny), F32)

    def vertical(e):
        keep = jnp.where(valid(e) & valid(e + 1), 1.0, 0.0).astype(F32)

        def body(r, carry):
            kz[e, pl.ds(pl.multiple_of(r * ROWS, ROWS), ROWS), :] = keep * (h[e, aligned(r), :] + h[e + 1, aligned(r), :])
            return carry

        lax.fori_loop(0, chunks, body, 0, unroll=chunks)

    def coefficients(p):
        def body(r, carry):
            at = pl.ds(pl.multiple_of(r * ROWS, ROWS), ROWS)
            here = h[p, aligned(r), :]
            x_next, x_prev = next_row(h, p, r, here), previous_row(h, p, r, here)
            y_next = jnp.where(lane < ny - 1, pltpu.roll(here, ny - 1, 1), 0.0)
            y_prev = jnp.where(lane > 0, pltpu.roll(here, 1, 1), 0.0)
            kxo[p, at, :] = here + x_next
            kxm[p, at, :] = here + x_prev
            kyo[p, at, :] = jnp.where(lane < ny - 1, here + y_next, 0.0)
            kym[p, at, :] = jnp.where(lane > 0, here + y_prev, 0.0)
            near = x_next + x_prev + y_next + y_prev
            diag[p, at, :] = 6.0 * here + near + h[p - 1, aligned(r), :] + h[p + 1, aligned(r), :]
            return carry

        lax.fori_loop(0, chunks, body, 0, unroll=chunks)

    def operate(src_v, dst_v, p, with_moments, sums):
        def body(r, carry):
            at = pl.ds(pl.multiple_of(r * ROWS, ROWS), ROWS)
            here = src_v[p, aligned(r), :]
            value = diag[p, at, :] * here
            value = value - kxo[p, at, :] * next_row(src_v, p, r, here)
            value = value - kxm[p, at, :] * previous_row(src_v, p, r, here)
            value = value - kyo[p, at, :] * pltpu.roll(here, ny - 1, 1)
            value = value - kym[p, at, :] * pltpu.roll(here, 1, 1)
            value = value - kz[p, at, :] * src_v[p + 1, aligned(r), :]
            value = value - kz[p - 1, at, :] * src_v[p - 1, aligned(r), :]
            dst_v[p, aligned(r), :] = value
            if not with_moments:
                return carry
            return (carry[0] + folded(here * value), carry[1] + folded(value * value))

        return lax.fori_loop(0, chunks, body, sums, unroll=chunks)

    def square(src_v, p, total):
        def body(r, carry):
            here = src_v[p, aligned(r), :]
            return carry + folded(here * here)

        return lax.fori_loop(0, chunks, body, total, unroll=chunks)

    def energy(field, p, total):
        def body(r, carry):
            at = pl.ds(pl.multiple_of(r * ROWS, ROWS), ROWS)
            here = field[p, aligned(r), :]
            near = kxo[p, at, :] * next_row(field, p, r, here)
            near = near + kyo[p, at, :] * pltpu.roll(here, ny - 1, 1)
            near = near + kz[p, at, :] * field[p + 1, aligned(r), :]
            return carry + folded(here * (diag[p, at, :] * here - 2.0 * near))

        return lax.fori_loop(0, chunks, body, total, unroll=chunks)

    nothing = jnp.zeros((ROWS, 128), F32)

    def krylov_own():
        m0 = square(v0, 3, square(v0, 2, nothing))
        return m0, operate(v0, v1, 3, True, operate(v0, v1, 2, True, (nothing, nothing)))

    def krylov_rest(m0, m12):
        for p in (1, 4, 5):
            operate(v0, v1, p, False, 0)
        m34 = operate(v1, v2, 3, True, operate(v1, v2, 2, True, (nothing, nothing)))
        operate(v1, v2, 4, False, 0)
        m5 = energy(v2, 3, energy(v2, 2, nothing))
        sums = [jnp.sum(jnp.sum(m, axis=0, keepdims=True), axis=1, keepdims=True) for m in (m0, *m12, *m34, m5)]
        place = lax.broadcasted_iota(jnp.int32, (1, 128), 1)
        row = jnp.zeros((1, 128), F32)
        for j, m in enumerate(sums):
            row = jnp.where(place == j, m, row)
        return row

    def share(source, landing, index):
        def start(k, carry):
            pltpu.make_async_remote_copy(
                src_ref=source, dst_ref=landing.at[s], send_sem=ar_send.at[index], recv_sem=ar_recv.at[index],
                device_id=(f, slab_at(k)), device_id_type=MESH,
            ).start()
            return carry

        lax.fori_loop(1, slabs, start, 0)

    def shared(landing, index):
        others = landing.at[pl.ds(0, slabs - 1)]
        whole = pltpu.make_async_remote_copy(
            src_ref=others, dst_ref=others, send_sem=ar_send.at[index], recv_sem=ar_recv.at[index],
            device_id=(f, slab_at(1)), device_id_type=MESH,
        )
        whole.wait_send()
        whole.wait_recv()

    def moments_of(landing):
        total = jnp.sum(landing[...], axis=0)
        return [total[:, j : j + 1] for j in range(6)]

    copy_h1.wait_recv()
    copy_h4.wait_recv()
    zero_outside(1)
    zero_outside(4)
    for e in (1, 2, 3):
        vertical(e)
    for p in (2, 3):
        coefficients(p)
    for copy in copies_q:
        copy.wait_recv()
    for c in range(4):
        prolong(c)
    m0, m12 = krylov_own()
    copy_h0.wait_recv()
    copy_h5.wait_recv()
    copy_h6.wait_recv()
    for p in (0, 5, 6):
        zero_outside(p)
    for e in (0, 4, 5):
        vertical(e)
    for p in (1, 4, 5):
        coefficients(p)
    moments = krylov_rest(m0, m12)
    msg[0] = moments
    got1[s] = moments
    share(msg.at[0], got1, 0)

    for j, field in enumerate((v0, v1, v2)):
        whole = jnp.concatenate([field[2, PAD : PAD + nx, :], field[3, PAD : PAD + nx, :]], axis=0)
        rows = sum(dot(gat[...], part) for part in parts_of(whole))
        column = jnp.sum(rows * hot_y[...].astype(F32), axis=1, keepdims=True)
        pmsg[j] = sublanes_to_lanes(column)
    p_sems = (p_send, p_recv)
    copies_p = [
        send(pmsg, pgot.at[0], p_sems, 0, (f, slab_at(1))),
        send(pmsg, pgot.at[1], p_sems, 1, (f, slab_at(-1))),
        send(pmsg, pgot.at[2], p_sems, 2, (f, slab_at(-2))),
    ]
    shared(got1, 0)
    c0, c1, c2 = cg_coefficients(moments_of(got1))
    observed = obs_ref[...]

    def misfit(values):
        return c0 * values[0] + c1 * values[1] + c2 * values[2] - observed

    mine = jnp.where(inside, misfit([pmsg[j] for j in range(3)]), 0.0)
    dmsg[...] = mine
    dgot[s] = mine
    share(dmsg, dgot, 1)
    for copy in copies_p:
        copy.wait_recv()
    d = misfit([pmsg[j] + pgot[0, j] + pgot[1, j] + pgot[2, j] for j in range(3)])

    d_parts = parts_of(d)
    for p in range(PLANES):
        hit = zx_row == lax.broadcasted_iota(jnp.int32, (nx, recv), 0) + p * nx
        value = sum(dot(jnp.where(hit, part.astype(F32), 0.0).astype(BF16), hot_y[...]) for part in d_parts)
        v0[p, PAD : PAD + nx, :] = jnp.where(valid(p), value, 0.0)
    moments = krylov_rest(*krylov_own())
    msg[1] = moments
    got2[s] = moments
    share(msg.at[1], got2, 2)
    shared(got2, 2)
    c0, c1, c2 = cg_coefficients(moments_of(got2))

    def restrict(r, carry):
        at = aligned(r)
        fine = [c0 * v0[p, at, :] + c1 * v1[p, at, :] + c2 * v2[p, at, :] for p in (2, 3)]
        both = fine[0] + fine[1]
        for t in range(ny // 128):
            tall[t, pl.ds(pl.multiple_of(r * ROWS, ROWS), ROWS), :] = both[:, t * 128 : t * 128 + 128]
        return carry

    lax.fori_loop(0, chunks, restrict, 0, unroll=chunks)
    pairs = jnp.concatenate(
        [tall[t, pl.ds(0, nxc, 2), :] + tall[t, pl.ds(1, nxc, 2), :] for t in range(ny // 128)], axis=1
    )
    down = (((1,), (1,)), ((), ()))
    wc[...] = sum(lax.dot_general(part, up[...], down, preferred_element_type=F32) for part in parts_of(pairs))

    def part_at(g):
        return pl.ds(pl.multiple_of(g * quarter, quarter), quarter)

    wg[f] = wc[part_at(f), :]
    y_sems = (y_send, y_recv)
    copies_w = [
        send(wc.at[part_at(frame_at(k)), :], wg.at[f], y_sems, k - 1, (frame_at(k), s)) for k in range(1, frames)
    ]
    for copy in copies_w:
        copy.wait_recv()
    inverse = smoothing_inverse(frames)
    for g in range(frames):
        uq[g] = sum(float(inverse[g, k]) * wg[k] for k in range(frames))
    uf[0, part_at(f), :] = uq[f]
    copies_u = []
    for k in range(frames):
        to = frame_at(k)
        copies_u.append(send(uq.at[to], uf.at[1, part_at(f), :], y_sems, 2 * frames + k, (to, slab_at(-1))))
        if k > 0:
            copies_u.append(send(uq.at[to], uf.at[0, part_at(f), :], y_sems, frames + k, (to, s)))
    shared(dgot, 1)
    misfit_ref[...] = jnp.sum(dgot[...], axis=0)
    for copy in copies_u:
        copy.wait_recv()
    u = uf[0]
    out_ref[0] = u - jnp.where(s < slabs - 1, uf[1], 0.0)
    out_ref[1] = u - jnp.where(row_c < nxc - 1, pltpu.roll(u, nxc - 1, 0), 0.0)
    out_ref[2] = u - jnp.where(lane_c < nyc - 1, pltpu.roll(u, nyc - 1, 1), 0.0)
    for copy in [copy_cz, copy_h0, copy_h1, copy_h4, copy_h5, copy_h6, *copies_q, *copies_p, *copies_w, *copies_u]:
        copy.wait_send()


def shards(frames, slabs, labels, region_conductivity, source, receivers, observed):
    _, nx, ny = labels.shape
    nxc, nyc = nx // 2, ny // 2
    recv = receivers.shape[2]
    quarter = nxc // frames
    vmem = pl.BlockSpec(memory_space=pltpu.VMEM)
    plane = (PLANES, nx, ny)
    padded = (PLANES, nx + 2 * PAD, ny)
    scratch = [
        pltpu.VMEM((2, nx, ny), jnp.int32),
        pltpu.VMEM((3, nxc, nyc), F32),
        *[pltpu.VMEM(padded, F32) for _ in range(4)],
        *[pltpu.VMEM(plane, F32) for _ in range(6)],
        pltpu.VMEM((nxc, nyc), F32),
        pltpu.VMEM((4, nxc, nyc), F32),
        pltpu.VMEM((nyc, ny), BF16),
        pltpu.VMEM((ny // 128, nx, 128), F32),
        pltpu.VMEM((recv, 2 * nx), BF16),
        pltpu.VMEM((recv, ny), BF16),
        pltpu.VMEM((2, 1, 128), F32),
        pltpu.VMEM((slabs, 1, 128), F32),
        pltpu.VMEM((slabs, 1, 128), F32),
        pltpu.VMEM((3, 1, recv), F32),
        pltpu.VMEM((3, 3, 1, recv), F32),
        pltpu.VMEM((1, recv), F32),
        pltpu.VMEM((slabs, 1, recv), F32),
        pltpu.VMEM((nxc, nyc), F32),
        pltpu.VMEM((frames, quarter, nyc), F32),
        pltpu.VMEM((frames, quarter, nyc), F32),
        pltpu.VMEM((2, nxc, nyc), F32),
        pltpu.SemaphoreType.DMA((2,)),
        *[pltpu.SemaphoreType.DMA((5,)) for _ in range(2)],
        *[pltpu.SemaphoreType.DMA((4,)) for _ in range(2)],
        *[pltpu.SemaphoreType.DMA((3,)) for _ in range(2)],
        *[pltpu.SemaphoreType.DMA((3,)) for _ in range(2)],
        *[pltpu.SemaphoreType.DMA((3 * frames,)) for _ in range(2)],
    ]
    out, misfit = pl.pallas_call(
        functools.partial(kernel, frames, slabs, region_conductivity.shape[0]),
        out_shape=(jax.ShapeDtypeStruct((3, nxc, nyc), F32), jax.ShapeDtypeStruct((1, recv), F32)),
        in_specs=[
            pl.BlockSpec(memory_space=pl.ANY),
            pl.BlockSpec(memory_space=pltpu.SMEM),
            pl.BlockSpec(memory_space=pl.ANY),
            vmem,
            vmem,
        ],
        out_specs=(vmem, vmem),
        scratch_shapes=scratch,
        compiler_params=pltpu.CompilerParams(
            collective_id=0, has_side_effects=True, vmem_limit_bytes=48 * 1024 * 1024
        ),
    )(labels, region_conductivity, source.reshape(3, nxc, nyc), receivers[0], observed)
    return out.reshape(1, 3, 1, nxc, nyc), misfit


def solution(mesh):
    in_specs = (
        P("space", None, None),
        P(),
        P("frame", None, "space", None, None),
        P("frame", None, None),
        P("frame", None),
    )
    out_specs = (P("frame", None, "space", None, None), P("frame", None))
    body = functools.partial(shards, mesh.shape["frame"], mesh.shape["space"])
    return jax.shard_map(body, mesh=mesh, in_specs=in_specs, out_specs=out_specs, check_vma=False)
```

```python
import functools

import jax
import jax.numpy as jnp
import numpy as np
from jax import lax
from jax.experimental import pallas as pl
from jax.experimental.pallas import tpu as pltpu
from jax.sharding import PartitionSpec as P

SMOOTHING = 4.0
PAD = 8
ROWS = 8
PLANES = 7
MESH = pl.DeviceIdType.MESH
F32 = jnp.float32
BF16 = jnp.bfloat16


def smoothing_inverse(frames):
    matrix = np.zeros((frames, frames))
    for f in range(frames):
        near = [g for g in (f - 1, f + 1) if 0 <= g < frames]
        matrix[f, f] = 1.0 + SMOOTHING * len(near)
        for g in near:
            matrix[f, g] = -SMOOTHING
    return np.linalg.inv(matrix)


def parts_of(x):
    high = x.astype(BF16)
    rest = x - high.astype(F32)
    middle = rest.astype(BF16)
    low = (rest - middle.astype(F32)).astype(BF16)
    return high, middle, low


def dot(a, b):
    return jnp.dot(a, b, preferred_element_type=F32)


def lanes_to_sublanes(row):
    n = row.shape[1]
    same = lax.broadcasted_iota(jnp.int32, (n, n), 0) == lax.broadcasted_iota(jnp.int32, (n, n), 1)
    return jnp.sum(jnp.where(same, row, jnp.zeros_like(row)), axis=1, keepdims=True)


def sublanes_to_lanes(column):
    n = column.shape[0]
    same = lax.broadcasted_iota(jnp.int32, (n, n), 0) == lax.broadcasted_iota(jnp.int32, (n, n), 1)
    return jnp.sum(jnp.where(same, column, jnp.zeros_like(column)), axis=0, keepdims=True)


def folded(x):
    total = x[:, :128]
    for start in range(128, x.shape[1], 128):
        total = total + x[:, start : start + 128]
    return total


def cg_coefficients(m):
    m0, m1, m2, m3, m4, m5 = m
    a0 = m0 / m1
    rr1 = m0 - 2.0 * a0 * m1 + a0 * a0 * m2
    b0 = rr1 / m0
    p0, p1 = 1.0 + b0, -a0
    a1 = rr1 / (p0 * p0 * m1 + 2.0 * p0 * p1 * m2 + p1 * p1 * m3)
    r0, r1, r2 = 1.0, -a0 - a1 * p0, -a1 * p1
    rr2 = m0 + r1 * r1 * m2 + r2 * r2 * m4 + 2.0 * (r1 * m1 + r2 * m2 + r1 * r2 * m3)
    b1 = rr2 / rr1
    q0, q1, q2 = r0 + b1 * p0, r1 + b1 * p1, r2
    curv = q0 * q0 * m1 + q1 * q1 * m3 + q2 * q2 * m5
    curv = curv + 2.0 * (q0 * q1 * m2 + q0 * q2 * m3 + q1 * q2 * m4)
    a2 = rr2 / curv
    return a0 + a1 * p0 + a2 * q0, a1 * p1 + a2 * q1, a2 * q2


def kernel(
    frames, slabs, regions,
    labels_ref, cond_ref, source_ref, recv_hbm, obs_hbm,
    out_ref, misfit_ref,
    lab, src, recv_ref, obs_ref, h, v0, v1, v2, diag, kxo, kxm, kyo, kym, kz,
    czb, qs, up, tall, gat, hot_y, msg, got1, got2, pmsg, pgot, dmsg, dgot, wc, wg, uq, uf,
    load_sem, h_send, h_recv, q_send, q_recv, ar_send, ar_recv, p_send, p_recv, y_send, y_recv,
):
    nx, ny = lab.shape[1], lab.shape[2]
    nxc, nyc = nx // 2, ny // 2
    recv = recv_ref.shape[1]
    quarter = nxc // frames
    chunks = nx // ROWS
    f = lax.axis_index("frame")
    s = lax.axis_index("space")

    def slab_at(by):
        return lax.rem(s + by + slabs, slabs)

    def frame_at(by):
        return lax.rem(f + by, frames)

    barrier = pltpu.get_barrier_semaphore()

    def greet(k, carry):
        pl.semaphore_signal(barrier, inc=1, device_id=(f, slab_at(k)), device_id_type=MESH)
        return carry

    lax.fori_loop(1, slabs, greet, 0)
    for k in range(1, frames):
        for by in (0, 1, -1):
            pl.semaphore_signal(barrier, inc=1, device_id=(frame_at(k), slab_at(by)), device_id_type=MESH)
    greeted = slabs - 1 + 3 * (frames - 1)

    load_labels = pltpu.make_async_copy(labels_ref, lab, load_sem.at[0])
    load_source = pltpu.make_async_copy(source_ref.at[0, :, 0], src, load_sem.at[1])
    load_labels.start()
    load_source.start()
    load_recv = pltpu.make_async_copy(recv_hbm.at[:, 0], recv_ref, load_sem.at[2])
    load_obs = pltpu.make_async_copy(obs_hbm, obs_ref, load_sem.at[3])
    load_recv.start()
    load_obs.start()

    zero_rows = jnp.zeros((PAD, ny), F32)
    for field in (h, v0, v1, v2):
        for p in range(PLANES):
            field[p, 0:PAD, :] = zero_rows
            field[p, PAD + nx : PAD + nx + PAD, :] = zero_rows
    load_recv.wait()
    load_obs.wait()
    first = 2 * s - 2
    zx_row = (recv_ref[0:1, :] - first) * nx + recv_ref[1:2, :]
    zx_col = lanes_to_sublanes(zx_row)
    y_col = lanes_to_sublanes(recv_ref[2:3, :])
    own_ids = lax.broadcasted_iota(jnp.int32, (recv, 2 * nx), 1) + 2 * nx
    gat[...] = (zx_col == own_ids).astype(BF16)
    hot_y[...] = (y_col == lax.broadcasted_iota(jnp.int32, (recv, ny), 1)).astype(BF16)
    coarse_id = lax.broadcasted_iota(jnp.int32, (nyc, ny), 0)
    up[...] = (coarse_id == lax.broadcasted_iota(jnp.int32, (nyc, ny), 1) // 2).astype(BF16)
    z_in = recv_ref[0:1, :] - 2 * s
    inside = (z_in >= 0) & (z_in < 2)

    load_labels.wait()

    def convert(i, carry):
        p, r = i // chunks, i % chunks
        here = lab[p, pl.ds(pl.multiple_of(r * ROWS, ROWS), ROWS), :]
        value = jnp.full((ROWS, ny), 0.5 * cond_ref[0], F32)
        for region in range(1, regions):
            value = jnp.where(here == region, 0.5 * cond_ref[region], value)
        h[p + 2, pl.ds(pl.multiple_of(PAD + r * ROWS, ROWS), ROWS), :] = value
        return carry

    lax.fori_loop(0, 2 * chunks, convert, 0, unroll=chunks)
    load_source.wait()

    pl.semaphore_wait(barrier, greeted)

    def remote(src_ref, dst_ref, sems, index, device):
        return pltpu.make_async_remote_copy(
            src_ref=src_ref, dst_ref=dst_ref, send_sem=sems[0].at[index], recv_sem=sems[1].at[index],
            device_id=device, device_id_type=MESH,
        )

    def send(*args):
        copy = remote(*args)
        copy.start()
        return copy

    def plane(p):
        return h.at[p, pl.ds(PAD, nx), :]

    def strip(p):
        rows = nx // frames
        return h.at[p, pl.ds(pl.multiple_of(PAD + f * rows, ROWS), rows), :]

    copy_cz = send(src.at[0], czb, (q_send, q_recv), 0, (f, slab_at(1)))
    h_sems = (h_send, h_recv)
    odd = lax.rem(s, 2) == 1
    copy_strip = remote(strip(2), strip(6), h_sems, 4, (f, slab_at(-2)))
    copies_strip = [remote(strip(6), strip(6), h_sems, 5 + k, (frame_at(k), s)) for k in range(1, frames)]
    copy_relay = remote(plane(4), plane(6), h_sems, 5, (f, slab_at(-1)))
    pl.when(odd)(copy_strip.start)
    copy_h1 = send(plane(3), plane(1), h_sems, 0, (f, slab_at(1)))
    copy_h4 = send(plane(2), plane(4), h_sems, 1, (f, slab_at(-1)))
    copy_h0 = send(plane(2), plane(0), h_sems, 2, (f, slab_at(1)))
    copy_h5 = send(plane(3), plane(5), h_sems, 3, (f, slab_at(-1)))

    row_c = lax.broadcasted_iota(jnp.int32, (nxc, nyc), 0)
    lane_c = lax.broadcasted_iota(jnp.int32, (nxc, nyc), 1)
    along_x, along_y = src[1], src[2]
    total = src[0] + along_x - jnp.where(row_c > 0, pltpu.roll(along_x, 1, 0), 0.0)
    total = total + along_y - jnp.where(lane_c > 0, pltpu.roll(along_y, 1, 1), 0.0)
    copy_cz.wait_recv()
    qs[1] = total - jnp.where(s > 0, czb[...], 0.0)
    q_sems = (q_send, q_recv)
    copies_q = [
        send(qs.at[1], qs.at[0], q_sems, 1, (f, slab_at(1))),
        send(qs.at[1], qs.at[2], q_sems, 2, (f, slab_at(-1))),
        send(qs.at[1], qs.at[3], q_sems, 3, (f, slab_at(-2))),
    ]

    def valid(p):
        z = first + p
        return (z >= 0) & (z < 2 * slabs)

    def aligned(r):
        return pl.ds(pl.multiple_of(PAD + r * ROWS, ROWS), ROWS)

    def next_row(field, p, r, here):
        return pltpu.roll(jnp.where(sub == 0, field[p, aligned(r + 1), :], here), ROWS - 1, 0)

    def previous_row(field, p, r, here):
        return pltpu.roll(jnp.where(sub == ROWS - 1, field[p, aligned(r - 1), :], here), 1, 0)

    def prolong(c):
        z = s - 1 + c
        ok = (z >= 0) & (z < slabs)
        high, middle, low = parts_of(jnp.where(ok, qs[c], 0.0))
        fine = dot(high, up[...]) + dot(middle, up[...]) + dot(low, up[...])
        for t in range(ny // 128):
            tall[t, pl.ds(0, nxc, 2), :] = fine[:, t * 128 : t * 128 + 128]
            tall[t, pl.ds(1, nxc, 2), :] = fine[:, t * 128 : t * 128 + 128]
        for p in (2 * c, 2 * c + 1):
            if p < PLANES:
                for t in range(ny // 128):
                    v0[p, PAD : PAD + nx, t * 128 : t * 128 + 128] = tall[t]

    lane = lax.broadcasted_iota(jnp.int32, (ROWS, ny), 1)
    sub = lax.broadcasted_iota(jnp.int32, (ROWS, ny), 0)

    def zero_outside(p):
        @pl.when(jnp.logical_not(valid(p)))
        def _():
            h[p, PAD : PAD + nx, :] = jnp.zeros((nx, ny), F32)

    def vertical(e):
        keep = jnp.where(valid(e) & valid(e + 1), 1.0, 0.0).astype(F32)

        def body(r, carry):
            kz[e, pl.ds(pl.multiple_of(r * ROWS, ROWS), ROWS), :] = keep * (h[e, aligned(r), :] + h[e + 1, aligned(r), :])
            return carry

        lax.fori_loop(0, chunks, body, 0, unroll=chunks)

    def coefficients(p):
        def body(r, carry):
            at = pl.ds(pl.multiple_of(r * ROWS, ROWS), ROWS)
            here = h[p, aligned(r), :]
            x_next, x_prev = next_row(h, p, r, here), previous_row(h, p, r, here)
            y_next = jnp.where(lane < ny - 1, pltpu.roll(here, ny - 1, 1), 0.0)
            y_prev = jnp.where(lane > 0, pltpu.roll(here, 1, 1), 0.0)
            kxo[p, at, :] = here + x_next
            kxm[p, at, :] = here + x_prev
            kyo[p, at, :] = jnp.where(lane < ny - 1, here + y_next, 0.0)
            kym[p, at, :] = jnp.where(lane > 0, here + y_prev, 0.0)
            near = x_next + x_prev + y_next + y_prev
            diag[p, at, :] = 6.0 * here + near + h[p - 1, aligned(r), :] + h[p + 1, aligned(r), :]
            return carry

        lax.fori_loop(0, chunks, body, 0, unroll=chunks)

    def operate(src_v, dst_v, p, with_moments, sums):
        def body(r, carry):
            at = pl.ds(pl.multiple_of(r * ROWS, ROWS), ROWS)
            here = src_v[p, aligned(r), :]
            value = diag[p, at, :] * here
            value = value - kxo[p, at, :] * next_row(src_v, p, r, here)
            value = value - kxm[p, at, :] * previous_row(src_v, p, r, here)
            value = value - kyo[p, at, :] * pltpu.roll(here, ny - 1, 1)
            value = value - kym[p, at, :] * pltpu.roll(here, 1, 1)
            value = value - kz[p, at, :] * src_v[p + 1, aligned(r), :]
            value = value - kz[p - 1, at, :] * src_v[p - 1, aligned(r), :]
            dst_v[p, aligned(r), :] = value
            if not with_moments:
                return carry
            return (carry[0] + folded(here * value), carry[1] + folded(value * value))

        return lax.fori_loop(0, chunks, body, sums, unroll=chunks)

    def square(src_v, p, total):
        def body(r, carry):
            here = src_v[p, aligned(r), :]
            return carry + folded(here * here)

        return lax.fori_loop(0, chunks, body, total, unroll=chunks)

    def energy(field, p, total):
        def body(r, carry):
            at = pl.ds(pl.multiple_of(r * ROWS, ROWS), ROWS)
            here = field[p, aligned(r), :]
            near = kxo[p, at, :] * next_row(field, p, r, here)
            near = near + kyo[p, at, :] * pltpu.roll(here, ny - 1, 1)
            near = near + kz[p, at, :] * field[p + 1, aligned(r), :]
            return carry + folded(here * (diag[p, at, :] * here - 2.0 * near))

        return lax.fori_loop(0, chunks, body, total, unroll=chunks)

    nothing = jnp.zeros((ROWS, 128), F32)

    def krylov_own():
        m0 = square(v0, 3, square(v0, 2, nothing))
        return m0, operate(v0, v1, 3, True, operate(v0, v1, 2, True, (nothing, nothing)))

    def krylov_near():
        for p in (1, 4):
            operate(v0, v1, p, False, 0)
        m34 = operate(v1, v2, 3, True, operate(v1, v2, 2, True, (nothing, nothing)))
        return m34, energy(v2, 2, nothing)

    def krylov_far(m5):
        operate(v0, v1, 5, False, 0)
        operate(v1, v2, 4, False, 0)
        return energy(v2, 3, m5)

    def summed(*moments):
        place = lax.broadcasted_iota(jnp.int32, (1, 128), 1)
        row = jnp.zeros((1, 128), F32)
        for j, m in enumerate(moments):
            row = jnp.where(place == j, jnp.sum(jnp.sum(m, axis=0, keepdims=True), axis=1, keepdims=True), row)
        return row

    def share(source, landing, index):
        def start(i, carry):
            k = lax.rem(i + slabs // 2, slabs - 1) + 1
            pltpu.make_async_remote_copy(
                src_ref=source, dst_ref=landing.at[s], send_sem=ar_send.at[index], recv_sem=ar_recv.at[index],
                device_id=(f, slab_at(k)), device_id_type=MESH,
            ).start()
            return carry

        lax.fori_loop(0, slabs - 1, start, 0)

    def shared(landing, index):
        others = landing.at[pl.ds(0, slabs - 1)]
        whole = pltpu.make_async_remote_copy(
            src_ref=others, dst_ref=others, send_sem=ar_send.at[index], recv_sem=ar_recv.at[index],
            device_id=(f, slab_at(1)), device_id_type=MESH,
        )
        whole.wait_send()
        whole.wait_recv()

    def moments_of(landing):
        total = jnp.sum(landing[...], axis=0)
        return [total[:, j : j + 1] for j in range(6)]

    @pl.when(odd)
    def _():
        copy_strip.wait_recv()
        for copy in copies_strip:
            copy.start()

    copy_h1.wait_recv()
    copy_h4.wait_recv()
    zero_outside(1)
    zero_outside(4)
    pl.when(odd)(copy_relay.start)
    for e in (1, 2, 3):
        vertical(e)
    for p in (2, 3):
        coefficients(p)
    for copy in copies_q:
        copy.wait_recv()
    for c in range(4):
        prolong(c)
    m0, m12 = krylov_own()
    copy_h0.wait_recv()
    copy_h5.wait_recv()
    zero_outside(0)
    zero_outside(5)
    vertical(0)
    vertical(4)
    coefficients(1)
    coefficients(4)
    m34, m5 = krylov_near()

    @pl.when(odd)
    def _():
        for copy in copies_strip:
            copy.wait()

    pl.when(jnp.logical_not(odd))(copy_relay.wait_recv)
    zero_outside(6)
    vertical(5)
    coefficients(5)
    m5 = krylov_far(m5)
    moments = summed(m0, *m12, *m34, m5)
    msg[0] = moments
    got1[s] = moments
    share(msg.at[0], got1, 0)

    for j, field in enumerate((v0, v1, v2)):
        whole = jnp.concatenate([field[2, PAD : PAD + nx, :], field[3, PAD : PAD + nx, :]], axis=0)
        rows = sum(dot(gat[...], part) for part in parts_of(whole))
        column = jnp.sum(rows * hot_y[...].astype(F32), axis=1, keepdims=True)
        pmsg[j] = sublanes_to_lanes(column)
    p_sems = (p_send, p_recv)
    copies_p = [
        send(pmsg, pgot.at[0], p_sems, 0, (f, slab_at(1))),
        send(pmsg, pgot.at[1], p_sems, 1, (f, slab_at(-1))),
        send(pmsg, pgot.at[2], p_sems, 2, (f, slab_at(-2))),
    ]
    shared(got1, 0)
    c0, c1, c2 = cg_coefficients(moments_of(got1))
    observed = obs_ref[...]

    def misfit(values):
        return c0 * values[0] + c1 * values[1] + c2 * values[2] - observed

    mine = jnp.where(inside, misfit([pmsg[j] for j in range(3)]), 0.0)
    dmsg[...] = mine
    dgot[s] = mine
    share(dmsg, dgot, 1)
    for copy in copies_p:
        copy.wait_recv()
    d = misfit([pmsg[j] + pgot[0, j] + pgot[1, j] + pgot[2, j] for j in range(3)])

    d_parts = parts_of(d)
    for p in range(PLANES):
        hit = zx_row == lax.broadcasted_iota(jnp.int32, (nx, recv), 0) + p * nx
        value = sum(dot(jnp.where(hit, part.astype(F32), 0.0).astype(BF16), hot_y[...]) for part in d_parts)
        v0[p, PAD : PAD + nx, :] = jnp.where(valid(p), value, 0.0)
    m0, m12 = krylov_own()
    m34, m5 = krylov_near()
    moments = summed(m0, *m12, *m34, krylov_far(m5))
    msg[1] = moments
    got2[s] = moments
    share(msg.at[1], got2, 2)
    shared(got2, 2)
    c0, c1, c2 = cg_coefficients(moments_of(got2))

    def restrict(r, carry):
        at = aligned(r)
        fine = [c0 * v0[p, at, :] + c1 * v1[p, at, :] + c2 * v2[p, at, :] for p in (2, 3)]
        both = fine[0] + fine[1]
        for t in range(ny // 128):
            tall[t, pl.ds(pl.multiple_of(r * ROWS, ROWS), ROWS), :] = both[:, t * 128 : t * 128 + 128]
        return carry

    lax.fori_loop(0, chunks, restrict, 0, unroll=chunks)
    pairs = jnp.concatenate(
        [tall[t, pl.ds(0, nxc, 2), :] + tall[t, pl.ds(1, nxc, 2), :] for t in range(ny // 128)], axis=1
    )
    down = (((1,), (1,)), ((), ()))
    wc[...] = sum(lax.dot_general(part, up[...], down, preferred_element_type=F32) for part in parts_of(pairs))

    def part_at(g):
        return pl.ds(pl.multiple_of(g * quarter, quarter), quarter)

    wg[f] = wc[part_at(f), :]
    y_sems = (y_send, y_recv)
    copies_w = [
        send(wc.at[part_at(frame_at(k)), :], wg.at[f], y_sems, k - 1, (frame_at(k), s)) for k in range(1, frames)
    ]
    for copy in copies_w:
        copy.wait_recv()
    inverse = smoothing_inverse(frames)
    for g in range(frames):
        uq[g] = sum(float(inverse[g, k]) * wg[k] for k in range(frames))
    uf[0, part_at(f), :] = uq[f]
    copies_u = []
    for k in range(frames):
        to = frame_at(k)
        copies_u.append(send(uq.at[to], uf.at[1, part_at(f), :], y_sems, 2 * frames + k, (to, slab_at(-1))))
        if k > 0:
            copies_u.append(send(uq.at[to], uf.at[0, part_at(f), :], y_sems, frames + k, (to, s)))
    shared(dgot, 1)
    misfit_ref[...] = jnp.sum(dgot[...], axis=0)
    for copy in copies_u:
        copy.wait_recv()
    u = uf[0]
    out_ref[0] = u - jnp.where(s < slabs - 1, uf[1], 0.0)
    out_ref[1] = u - jnp.where(row_c < nxc - 1, pltpu.roll(u, nxc - 1, 0), 0.0)
    out_ref[2] = u - jnp.where(lane_c < nyc - 1, pltpu.roll(u, nyc - 1, 1), 0.0)
    @pl.when(odd)
    def _():
        for copy in [copy_strip, copy_relay]:
            copy.wait_send()

    for copy in [copy_cz, copy_h0, copy_h1, copy_h4, copy_h5, *copies_q, *copies_p, *copies_w, *copies_u]:
        copy.wait_send()


def shards(frames, slabs, labels, region_conductivity, source, receivers, observed):
    _, nx, ny = labels.shape
    nxc, nyc = nx // 2, ny // 2
    recv = receivers.shape[2]
    quarter = nxc // frames
    vmem = pl.BlockSpec(memory_space=pltpu.VMEM)
    hbm = pl.BlockSpec(memory_space=pltpu.HBM)
    plane = (PLANES, nx, ny)
    padded = (PLANES, nx + 2 * PAD, ny)
    scratch = [
        pltpu.VMEM((2, nx, ny), jnp.int32),
        pltpu.VMEM((3, nxc, nyc), F32),
        pltpu.VMEM((3, recv), jnp.int32),
        pltpu.VMEM((1, recv), F32),
        *[pltpu.VMEM(padded, F32) for _ in range(4)],
        *[pltpu.VMEM(plane, F32) for _ in range(6)],
        pltpu.VMEM((nxc, nyc), F32),
        pltpu.VMEM((4, nxc, nyc), F32),
        pltpu.VMEM((nyc, ny), BF16),
        pltpu.VMEM((ny // 128, nx, 128), F32),
        pltpu.VMEM((recv, 2 * nx), BF16),
        pltpu.VMEM((recv, ny), BF16),
        pltpu.VMEM((2, 1, 128), F32),
        pltpu.VMEM((slabs, 1, 128), F32),
        pltpu.VMEM((slabs, 1, 128), F32),
        pltpu.VMEM((3, 1, recv), F32),
        pltpu.VMEM((3, 3, 1, recv), F32),
        pltpu.VMEM((1, recv), F32),
        pltpu.VMEM((slabs, 1, recv), F32),
        pltpu.VMEM((nxc, nyc), F32),
        pltpu.VMEM((frames, quarter, nyc), F32),
        pltpu.VMEM((frames, quarter, nyc), F32),
        pltpu.VMEM((2, nxc, nyc), F32),
        pltpu.SemaphoreType.DMA((4,)),
        *[pltpu.SemaphoreType.DMA((5 + frames,)) for _ in range(2)],
        *[pltpu.SemaphoreType.DMA((4,)) for _ in range(2)],
        *[pltpu.SemaphoreType.DMA((3,)) for _ in range(2)],
        *[pltpu.SemaphoreType.DMA((3,)) for _ in range(2)],
        *[pltpu.SemaphoreType.DMA((3 * frames,)) for _ in range(2)],
    ]
    out, misfit = pl.pallas_call(
        functools.partial(kernel, frames, slabs, region_conductivity.shape[0]),
        out_shape=(jax.ShapeDtypeStruct((3, nxc, nyc), F32), jax.ShapeDtypeStruct((1, recv), F32)),
        in_specs=[hbm, pl.BlockSpec(memory_space=pltpu.SMEM), hbm, hbm, hbm],
        out_specs=(vmem, vmem),
        scratch_shapes=scratch,
        compiler_params=pltpu.CompilerParams(
            collective_id=0, has_side_effects=True, vmem_limit_bytes=64 * 1024 * 1024
        ),
    )(labels, region_conductivity, source, jnp.transpose(receivers, (1, 0, 2)), observed)
    return out.reshape(1, 3, 1, nxc, nyc), misfit


def solution(mesh):
    in_specs = (
        P("space", None, None),
        P(),
        P("frame", None, "space", None, None),
        P("frame", None, None),
        P("frame", None),
    )
    out_specs = (P("frame", None, "space", None, None), P("frame", None))
    body = functools.partial(shards, mesh.shape["frame"], mesh.shape["space"])
    return jax.shard_map(body, mesh=mesh, in_specs=in_specs, out_specs=out_specs, check_vma=False)
```

```python
import functools

import jax
import jax.numpy as jnp
import numpy as np
from jax import lax
from jax.experimental import pallas as pl
from jax.experimental.pallas import tpu as pltpu
from jax.sharding import PartitionSpec as P

SMOOTHING = 4.0
PAD = 8
ROWS = 8
PLANES = 7
MESH = pl.DeviceIdType.MESH
F32 = jnp.float32
BF16 = jnp.bfloat16


def smoothing_inverse(frames):
    matrix = np.zeros((frames, frames))
    for f in range(frames):
        near = [g for g in (f - 1, f + 1) if 0 <= g < frames]
        matrix[f, f] = 1.0 + SMOOTHING * len(near)
        for g in near:
            matrix[f, g] = -SMOOTHING
    return np.linalg.inv(matrix)


def parts_of(x):
    high = x.astype(BF16)
    rest = x - high.astype(F32)
    middle = rest.astype(BF16)
    low = (rest - middle.astype(F32)).astype(BF16)
    return high, middle, low


def dot(a, b):
    return jnp.dot(a, b, preferred_element_type=F32)


def lanes_to_sublanes(row):
    n = row.shape[1]
    same = lax.broadcasted_iota(jnp.int32, (n, n), 0) == lax.broadcasted_iota(jnp.int32, (n, n), 1)
    return jnp.sum(jnp.where(same, row, jnp.zeros_like(row)), axis=1, keepdims=True)


def sublanes_to_lanes(column):
    n = column.shape[0]
    same = lax.broadcasted_iota(jnp.int32, (n, n), 0) == lax.broadcasted_iota(jnp.int32, (n, n), 1)
    return jnp.sum(jnp.where(same, column, jnp.zeros_like(column)), axis=0, keepdims=True)


def folded(x):
    total = x[:, :128]
    for start in range(128, x.shape[1], 128):
        total = total + x[:, start : start + 128]
    return total


def cg_coefficients(m):
    m0, m1, m2, m3, m4, m5 = m
    a0 = m0 / m1
    rr1 = m0 - 2.0 * a0 * m1 + a0 * a0 * m2
    b0 = rr1 / m0
    p0, p1 = 1.0 + b0, -a0
    a1 = rr1 / (p0 * p0 * m1 + 2.0 * p0 * p1 * m2 + p1 * p1 * m3)
    r0, r1, r2 = 1.0, -a0 - a1 * p0, -a1 * p1
    rr2 = m0 + r1 * r1 * m2 + r2 * r2 * m4 + 2.0 * (r1 * m1 + r2 * m2 + r1 * r2 * m3)
    b1 = rr2 / rr1
    q0, q1, q2 = r0 + b1 * p0, r1 + b1 * p1, r2
    curv = q0 * q0 * m1 + q1 * q1 * m3 + q2 * q2 * m5
    curv = curv + 2.0 * (q0 * q1 * m2 + q0 * q2 * m3 + q1 * q2 * m4)
    a2 = rr2 / curv
    return a0 + a1 * p0 + a2 * q0, a1 * p1 + a2 * q1, a2 * q2


def kernel(
    frames, slabs, regions,
    labels_ref, cond_ref, source_ref, recv_hbm, obs_hbm,
    out_ref, misfit_ref,
    lab, src, recv_ref, obs_ref, h, v0, v1, v2, diag, kxo, kxm, kyo, kym, kz,
    czb, qs, up, tall, gat, hot_y, msg, got1, got2, pmsg, pgot, dmsg, dgot, wc, wg, uq, uf,
    load_sem, h_send, h_recv, q_send, q_recv, ar_send, ar_recv, p_send, p_recv, y_send, y_recv, known,
):
    nx, ny = lab.shape[1], lab.shape[2]
    nxc, nyc = nx // 2, ny // 2
    recv = recv_ref.shape[1]
    quarter = nxc // frames
    chunks = nx // ROWS
    f = lax.axis_index("frame")
    s = lax.axis_index("space")

    def slab_at(by):
        return lax.rem(s + by + slabs, slabs)

    def frame_at(by):
        return lax.rem(f + by, frames)

    barrier = pltpu.get_barrier_semaphore()

    def tell(semaphore, slabs_by, others):
        for by in slabs_by:
            pl.semaphore_signal(semaphore, inc=1, device_id=(f, slab_at(by)), device_id_type=MESH)
        if others:
            for k in range(1, frames):
                pl.semaphore_signal(semaphore, inc=1, device_id=(frame_at(k), s), device_id_type=MESH)
        return len(slabs_by) + (frames - 1 if others else 0)

    reach = slabs // 16
    quarters = [slabs // 4, slabs // 2, slabs - slabs // 4]
    near = [by for k in range(1, reach + 1) for by in (k, -k)]
    greeted = tell(barrier, near + quarters, True)

    load_labels = pltpu.make_async_copy(labels_ref, lab, load_sem.at[0])
    load_source = pltpu.make_async_copy(source_ref.at[0, :, 0], src, load_sem.at[1])
    load_labels.start()
    load_source.start()
    load_recv = pltpu.make_async_copy(recv_hbm.at[:, 0], recv_ref, load_sem.at[2])
    load_obs = pltpu.make_async_copy(obs_hbm, obs_ref, load_sem.at[3])
    load_recv.start()
    load_obs.start()

    load_labels.wait()

    def convert(i, carry):
        p, r = i // chunks, i % chunks
        here = lab[p, pl.ds(pl.multiple_of(r * ROWS, ROWS), ROWS), :]
        value = jnp.full((ROWS, ny), 0.5 * cond_ref[0], F32)
        for region in range(1, regions):
            value = jnp.where(here == region, 0.5 * cond_ref[region], value)
        h[p + 2, pl.ds(pl.multiple_of(PAD + r * ROWS, ROWS), ROWS), :] = value
        return carry

    lax.fori_loop(0, 2 * chunks, convert, 0, unroll=chunks)
    load_source.wait()

    pl.semaphore_wait(barrier, greeted)
    heard = tell(known.at[0], [reach, -reach], True)

    def remote(src_ref, dst_ref, sems, index, device):
        return pltpu.make_async_remote_copy(
            src_ref=src_ref, dst_ref=dst_ref, send_sem=sems[0].at[index], recv_sem=sems[1].at[index],
            device_id=device, device_id_type=MESH,
        )

    def send(*args):
        copy = remote(*args)
        copy.start()
        return copy

    def plane(p):
        return h.at[p, pl.ds(PAD, nx), :]

    def strip(p):
        rows = nx // frames
        return h.at[p, pl.ds(pl.multiple_of(PAD + f * rows, ROWS), rows), :]

    copy_cz = send(src.at[0], czb, (q_send, q_recv), 0, (f, slab_at(1)))
    h_sems = (h_send, h_recv)
    odd = lax.rem(s, 2) == 1
    copy_strip = remote(strip(2), strip(6), h_sems, 4, (f, slab_at(-2)))
    copies_strip = [remote(strip(6), strip(6), h_sems, 5 + k, (frame_at(k), s)) for k in range(1, frames)]
    copy_relay = remote(plane(4), plane(6), h_sems, 5, (f, slab_at(-1)))
    pl.when(odd)(copy_strip.start)
    copy_h1 = send(plane(3), plane(1), h_sems, 0, (f, slab_at(1)))
    copy_h4 = send(plane(2), plane(4), h_sems, 1, (f, slab_at(-1)))
    copy_h0 = send(plane(2), plane(0), h_sems, 2, (f, slab_at(1)))
    copy_h5 = send(plane(3), plane(5), h_sems, 3, (f, slab_at(-1)))

    row_c = lax.broadcasted_iota(jnp.int32, (nxc, nyc), 0)
    lane_c = lax.broadcasted_iota(jnp.int32, (nxc, nyc), 1)
    along_x, along_y = src[1], src[2]
    total = src[0] + along_x - jnp.where(row_c > 0, pltpu.roll(along_x, 1, 0), 0.0)
    total = total + along_y - jnp.where(lane_c > 0, pltpu.roll(along_y, 1, 1), 0.0)
    copy_cz.wait_recv()
    qs[1] = total - jnp.where(s > 0, czb[...], 0.0)
    q_sems = (q_send, q_recv)
    copies_q = [
        send(qs.at[1], qs.at[0], q_sems, 1, (f, slab_at(1))),
        send(qs.at[1], qs.at[2], q_sems, 2, (f, slab_at(-1))),
        send(qs.at[1], qs.at[3], q_sems, 3, (f, slab_at(-2))),
    ]

    zero_rows = jnp.zeros((PAD, ny), F32)
    for field in (h, v0, v1, v2):
        for p in range(PLANES):
            field[p, 0:PAD, :] = zero_rows
            field[p, PAD + nx : PAD + nx + PAD, :] = zero_rows
    load_recv.wait()
    load_obs.wait()
    first = 2 * s - 2
    zx_row = (recv_ref[0:1, :] - first) * nx + recv_ref[1:2, :]
    zx_col = lanes_to_sublanes(zx_row)
    y_col = lanes_to_sublanes(recv_ref[2:3, :])
    own_ids = lax.broadcasted_iota(jnp.int32, (recv, 2 * nx), 1) + 2 * nx
    gat[...] = (zx_col == own_ids).astype(BF16)
    hot_y[...] = (y_col == lax.broadcasted_iota(jnp.int32, (recv, ny), 1)).astype(BF16)
    coarse_id = lax.broadcasted_iota(jnp.int32, (nyc, ny), 0)
    up[...] = (coarse_id == lax.broadcasted_iota(jnp.int32, (nyc, ny), 1) // 2).astype(BF16)
    z_in = recv_ref[0:1, :] - 2 * s
    inside = (z_in >= 0) & (z_in < 2)

    def valid(p):
        z = first + p
        return (z >= 0) & (z < 2 * slabs)

    def aligned(r):
        return pl.ds(pl.multiple_of(PAD + r * ROWS, ROWS), ROWS)

    def next_row(field, p, r, here):
        return pltpu.roll(jnp.where(sub == 0, field[p, aligned(r + 1), :], here), ROWS - 1, 0)

    def previous_row(field, p, r, here):
        return pltpu.roll(jnp.where(sub == ROWS - 1, field[p, aligned(r - 1), :], here), 1, 0)

    def prolong(c):
        z = s - 1 + c
        ok = (z >= 0) & (z < slabs)
        high, middle, low = parts_of(jnp.where(ok, qs[c], 0.0))
        fine = dot(high, up[...]) + dot(middle, up[...]) + dot(low, up[...])
        for t in range(ny // 128):
            tall[t, pl.ds(0, nxc, 2), :] = fine[:, t * 128 : t * 128 + 128]
            tall[t, pl.ds(1, nxc, 2), :] = fine[:, t * 128 : t * 128 + 128]
        for p in (2 * c, 2 * c + 1):
            if p < PLANES:
                for t in range(ny // 128):
                    v0[p, PAD : PAD + nx, t * 128 : t * 128 + 128] = tall[t]

    lane = lax.broadcasted_iota(jnp.int32, (ROWS, ny), 1)
    sub = lax.broadcasted_iota(jnp.int32, (ROWS, ny), 0)

    def zero_outside(p):
        @pl.when(jnp.logical_not(valid(p)))
        def _():
            h[p, PAD : PAD + nx, :] = jnp.zeros((nx, ny), F32)

    def vertical(e):
        keep = jnp.where(valid(e) & valid(e + 1), 1.0, 0.0).astype(F32)

        def body(r, carry):
            kz[e, pl.ds(pl.multiple_of(r * ROWS, ROWS), ROWS), :] = keep * (h[e, aligned(r), :] + h[e + 1, aligned(r), :])
            return carry

        lax.fori_loop(0, chunks, body, 0, unroll=chunks)

    def coefficients(p):
        def body(r, carry):
            at = pl.ds(pl.multiple_of(r * ROWS, ROWS), ROWS)
            here = h[p, aligned(r), :]
            x_next, x_prev = next_row(h, p, r, here), previous_row(h, p, r, here)
            y_next = jnp.where(lane < ny - 1, pltpu.roll(here, ny - 1, 1), 0.0)
            y_prev = jnp.where(lane > 0, pltpu.roll(here, 1, 1), 0.0)
            kxo[p, at, :] = here + x_next
            kxm[p, at, :] = here + x_prev
            kyo[p, at, :] = jnp.where(lane < ny - 1, here + y_next, 0.0)
            kym[p, at, :] = jnp.where(lane > 0, here + y_prev, 0.0)
            near = x_next + x_prev + y_next + y_prev
            diag[p, at, :] = 6.0 * here + near + h[p - 1, aligned(r), :] + h[p + 1, aligned(r), :]
            return carry

        lax.fori_loop(0, chunks, body, 0, unroll=chunks)

    def operate(src_v, dst_v, p, with_moments, sums):
        def body(r, carry):
            at = pl.ds(pl.multiple_of(r * ROWS, ROWS), ROWS)
            here = src_v[p, aligned(r), :]
            value = diag[p, at, :] * here
            value = value - kxo[p, at, :] * next_row(src_v, p, r, here)
            value = value - kxm[p, at, :] * previous_row(src_v, p, r, here)
            value = value - kyo[p, at, :] * pltpu.roll(here, ny - 1, 1)
            value = value - kym[p, at, :] * pltpu.roll(here, 1, 1)
            value = value - kz[p, at, :] * src_v[p + 1, aligned(r), :]
            value = value - kz[p - 1, at, :] * src_v[p - 1, aligned(r), :]
            dst_v[p, aligned(r), :] = value
            if not with_moments:
                return carry
            return (carry[0] + folded(here * value), carry[1] + folded(value * value))

        return lax.fori_loop(0, chunks, body, sums, unroll=chunks)

    def square(src_v, p, total):
        def body(r, carry):
            here = src_v[p, aligned(r), :]
            return carry + folded(here * here)

        return lax.fori_loop(0, chunks, body, total, unroll=chunks)

    def energy(field, p, total):
        def body(r, carry):
            at = pl.ds(pl.multiple_of(r * ROWS, ROWS), ROWS)
            here = field[p, aligned(r), :]
            near = kxo[p, at, :] * next_row(field, p, r, here)
            near = near + kyo[p, at, :] * pltpu.roll(here, ny - 1, 1)
            near = near + kz[p, at, :] * field[p + 1, aligned(r), :]
            return carry + folded(here * (diag[p, at, :] * here - 2.0 * near))

        return lax.fori_loop(0, chunks, body, total, unroll=chunks)

    nothing = jnp.zeros((ROWS, 128), F32)

    def krylov_own():
        m0 = square(v0, 3, square(v0, 2, nothing))
        return m0, operate(v0, v1, 3, True, operate(v0, v1, 2, True, (nothing, nothing)))

    def krylov_near():
        for p in (1, 4):
            operate(v0, v1, p, False, 0)
        m34 = operate(v1, v2, 3, True, operate(v1, v2, 2, True, (nothing, nothing)))
        return m34, energy(v2, 2, nothing)

    def krylov_far(m5):
        operate(v0, v1, 5, False, 0)
        operate(v1, v2, 4, False, 0)
        return energy(v2, 3, m5)

    def summed(*moments):
        place = lax.broadcasted_iota(jnp.int32, (1, 128), 1)
        row = jnp.zeros((1, 128), F32)
        for j, m in enumerate(moments):
            row = jnp.where(place == j, jnp.sum(jnp.sum(m, axis=0, keepdims=True), axis=1, keepdims=True), row)
        return row

    def share(source, landing, index):
        def start(i, carry):
            k = lax.rem(i + slabs // 2, slabs - 1) + 1
            pltpu.make_async_remote_copy(
                src_ref=source, dst_ref=landing.at[s], send_sem=ar_send.at[index], recv_sem=ar_recv.at[index],
                device_id=(f, slab_at(k)), device_id_type=MESH,
            ).start()
            return carry

        lax.fori_loop(0, slabs - 1, start, 0)

    def shared(landing, index):
        others = landing.at[pl.ds(0, slabs - 1)]
        whole = pltpu.make_async_remote_copy(
            src_ref=others, dst_ref=others, send_sem=ar_send.at[index], recv_sem=ar_recv.at[index],
            device_id=(f, slab_at(1)), device_id_type=MESH,
        )
        whole.wait_send()
        whole.wait_recv()

    def moments_of(landing):
        total = jnp.sum(landing[...], axis=0)
        return [total[:, j : j + 1] for j in range(6)]

    @pl.when(odd)
    def _():
        copy_strip.wait_recv()
        for copy in copies_strip:
            copy.start()

    copy_h1.wait_recv()
    copy_h4.wait_recv()
    zero_outside(1)
    zero_outside(4)
    pl.when(odd)(copy_relay.start)
    for e in (1, 2, 3):
        vertical(e)
    for p in (2, 3):
        coefficients(p)
    for copy in copies_q:
        copy.wait_recv()
    for c in range(4):
        prolong(c)
    m0, m12 = krylov_own()
    pl.semaphore_wait(known.at[0], heard)
    heard = tell(known.at[1], quarters, False)
    copy_h0.wait_recv()
    copy_h5.wait_recv()
    zero_outside(0)
    zero_outside(5)
    vertical(0)
    vertical(4)
    coefficients(1)
    coefficients(4)
    m34, m5 = krylov_near()

    @pl.when(odd)
    def _():
        for copy in copies_strip:
            copy.wait()

    pl.when(jnp.logical_not(odd))(copy_relay.wait_recv)
    zero_outside(6)
    vertical(5)
    coefficients(5)
    m5 = krylov_far(m5)
    moments = summed(m0, *m12, *m34, m5)
    msg[0] = moments
    got1[s] = moments
    pl.semaphore_wait(known.at[1], heard)
    share(msg.at[0], got1, 0)

    for j, field in enumerate((v0, v1, v2)):
        whole = jnp.concatenate([field[2, PAD : PAD + nx, :], field[3, PAD : PAD + nx, :]], axis=0)
        rows = sum(dot(gat[...], part) for part in parts_of(whole))
        column = jnp.sum(rows * hot_y[...].astype(F32), axis=1, keepdims=True)
        pmsg[j] = sublanes_to_lanes(column)
    p_sems = (p_send, p_recv)
    copies_p = [
        send(pmsg, pgot.at[0], p_sems, 0, (f, slab_at(1))),
        send(pmsg, pgot.at[1], p_sems, 1, (f, slab_at(-1))),
        send(pmsg, pgot.at[2], p_sems, 2, (f, slab_at(-2))),
    ]
    shared(got1, 0)
    c0, c1, c2 = cg_coefficients(moments_of(got1))
    observed = obs_ref[...]

    def misfit(values):
        return c0 * values[0] + c1 * values[1] + c2 * values[2] - observed

    mine = jnp.where(inside, misfit([pmsg[j] for j in range(3)]), 0.0)
    dmsg[...] = mine
    dgot[s] = mine
    share(dmsg, dgot, 1)
    for copy in copies_p:
        copy.wait_recv()
    d = misfit([pmsg[j] + pgot[0, j] + pgot[1, j] + pgot[2, j] for j in range(3)])

    d_parts = parts_of(d)
    for p in range(PLANES):
        hit = zx_row == lax.broadcasted_iota(jnp.int32, (nx, recv), 0) + p * nx
        value = sum(dot(jnp.where(hit, part.astype(F32), 0.0).astype(BF16), hot_y[...]) for part in d_parts)
        v0[p, PAD : PAD + nx, :] = jnp.where(valid(p), value, 0.0)
    m0, m12 = krylov_own()
    m34, m5 = krylov_near()
    moments = summed(m0, *m12, *m34, krylov_far(m5))
    msg[1] = moments
    got2[s] = moments
    share(msg.at[1], got2, 2)
    shared(got2, 2)
    c0, c1, c2 = cg_coefficients(moments_of(got2))

    def restrict(r, carry):
        at = aligned(r)
        fine = [c0 * v0[p, at, :] + c1 * v1[p, at, :] + c2 * v2[p, at, :] for p in (2, 3)]
        both = fine[0] + fine[1]
        for t in range(ny // 128):
            tall[t, pl.ds(pl.multiple_of(r * ROWS, ROWS), ROWS), :] = both[:, t * 128 : t * 128 + 128]
        return carry

    lax.fori_loop(0, chunks, restrict, 0, unroll=chunks)
    pairs = jnp.concatenate(
        [tall[t, pl.ds(0, nxc, 2), :] + tall[t, pl.ds(1, nxc, 2), :] for t in range(ny // 128)], axis=1
    )
    down = (((1,), (1,)), ((), ()))
    wc[...] = sum(lax.dot_general(part, up[...], down, preferred_element_type=F32) for part in parts_of(pairs))

    def part_at(g):
        return pl.ds(pl.multiple_of(g * quarter, quarter), quarter)

    wg[f] = wc[part_at(f), :]
    y_sems = (y_send, y_recv)
    copies_w = [
        send(wc.at[part_at(frame_at(k)), :], wg.at[f], y_sems, k - 1, (frame_at(k), s)) for k in range(1, frames)
    ]
    for copy in copies_w:
        copy.wait_recv()
    inverse = smoothing_inverse(frames)
    for g in range(frames):
        uq[g] = sum(float(inverse[g, k]) * wg[k] for k in range(frames))
    uf[0, part_at(f), :] = uq[f]
    copies_u = []
    for k in range(frames):
        to = frame_at(k)
        copies_u.append(send(uq.at[to], uf.at[1, part_at(f), :], y_sems, 2 * frames + k, (to, slab_at(-1))))
        if k > 0:
            copies_u.append(send(uq.at[to], uf.at[0, part_at(f), :], y_sems, frames + k, (to, s)))
    shared(dgot, 1)
    misfit_ref[...] = jnp.sum(dgot[...], axis=0)
    for copy in copies_u:
        copy.wait_recv()
    u = uf[0]
    out_ref[0] = u - jnp.where(s < slabs - 1, uf[1], 0.0)
    out_ref[1] = u - jnp.where(row_c < nxc - 1, pltpu.roll(u, nxc - 1, 0), 0.0)
    out_ref[2] = u - jnp.where(lane_c < nyc - 1, pltpu.roll(u, nyc - 1, 1), 0.0)
    @pl.when(odd)
    def _():
        for copy in [copy_strip, copy_relay]:
            copy.wait_send()

    for copy in [copy_cz, copy_h0, copy_h1, copy_h4, copy_h5, *copies_q, *copies_p, *copies_w, *copies_u]:
        copy.wait_send()


def shards(frames, slabs, labels, region_conductivity, source, receivers, observed):
    _, nx, ny = labels.shape
    nxc, nyc = nx // 2, ny // 2
    recv = receivers.shape[2]
    quarter = nxc // frames
    vmem = pl.BlockSpec(memory_space=pltpu.VMEM)
    hbm = pl.BlockSpec(memory_space=pltpu.HBM)
    plane = (PLANES, nx, ny)
    padded = (PLANES, nx + 2 * PAD, ny)
    scratch = [
        pltpu.VMEM((2, nx, ny), jnp.int32),
        pltpu.VMEM((3, nxc, nyc), F32),
        pltpu.VMEM((3, recv), jnp.int32),
        pltpu.VMEM((1, recv), F32),
        *[pltpu.VMEM(padded, F32) for _ in range(4)],
        *[pltpu.VMEM(plane, F32) for _ in range(6)],
        pltpu.VMEM((nxc, nyc), F32),
        pltpu.VMEM((4, nxc, nyc), F32),
        pltpu.VMEM((nyc, ny), BF16),
        pltpu.VMEM((ny // 128, nx, 128), F32),
        pltpu.VMEM((recv, 2 * nx), BF16),
        pltpu.VMEM((recv, ny), BF16),
        pltpu.VMEM((2, 1, 128), F32),
        pltpu.VMEM((slabs, 1, 128), F32),
        pltpu.VMEM((slabs, 1, 128), F32),
        pltpu.VMEM((3, 1, recv), F32),
        pltpu.VMEM((3, 3, 1, recv), F32),
        pltpu.VMEM((1, recv), F32),
        pltpu.VMEM((slabs, 1, recv), F32),
        pltpu.VMEM((nxc, nyc), F32),
        pltpu.VMEM((frames, quarter, nyc), F32),
        pltpu.VMEM((frames, quarter, nyc), F32),
        pltpu.VMEM((2, nxc, nyc), F32),
        pltpu.SemaphoreType.DMA((4,)),
        *[pltpu.SemaphoreType.DMA((5 + frames,)) for _ in range(2)],
        *[pltpu.SemaphoreType.DMA((4,)) for _ in range(2)],
        *[pltpu.SemaphoreType.DMA((3,)) for _ in range(2)],
        *[pltpu.SemaphoreType.DMA((3,)) for _ in range(2)],
        *[pltpu.SemaphoreType.DMA((3 * frames,)) for _ in range(2)],
        pltpu.SemaphoreType.REGULAR((2,)),
    ]
    out, misfit = pl.pallas_call(
        functools.partial(kernel, frames, slabs, region_conductivity.shape[0]),
        out_shape=(jax.ShapeDtypeStruct((3, nxc, nyc), F32), jax.ShapeDtypeStruct((1, recv), F32)),
        in_specs=[hbm, pl.BlockSpec(memory_space=pltpu.SMEM), hbm, hbm, hbm],
        out_specs=(vmem, vmem),
        scratch_shapes=scratch,
        compiler_params=pltpu.CompilerParams(
            collective_id=0, has_side_effects=True, vmem_limit_bytes=64 * 1024 * 1024
        ),
    )(labels, region_conductivity, source, jnp.transpose(receivers, (1, 0, 2)), observed)
    return out.reshape(1, 3, 1, nxc, nyc), misfit


def solution(mesh):
    in_specs = (
        P("space", None, None),
        P(),
        P("frame", None, "space", None, None),
        P("frame", None, None),
        P("frame", None),
    )
    out_specs = (P("frame", None, "space", None, None), P("frame", None))
    body = functools.partial(shards, mesh.shape["frame"], mesh.shape["space"])
    return jax.shard_map(body, mesh=mesh, in_specs=in_specs, out_specs=out_specs, check_vma=False)
```

```python
import functools

import jax
import jax.numpy as jnp
import numpy as np
from jax import lax
from jax.experimental import pallas as pl
from jax.experimental.pallas import tpu as pltpu
from jax.sharding import PartitionSpec as P

SMOOTHING = 4.0
PAD = 8
ROWS = 8
PLANES = 7
MESH = pl.DeviceIdType.MESH
F32 = jnp.float32
BF16 = jnp.bfloat16


def smoothing_inverse(frames):
    matrix = np.zeros((frames, frames))
    for f in range(frames):
        near = [g for g in (f - 1, f + 1) if 0 <= g < frames]
        matrix[f, f] = 1.0 + SMOOTHING * len(near)
        for g in near:
            matrix[f, g] = -SMOOTHING
    return np.linalg.inv(matrix)


def parts_of(x):
    high = x.astype(BF16)
    rest = x - high.astype(F32)
    middle = rest.astype(BF16)
    low = (rest - middle.astype(F32)).astype(BF16)
    return high, middle, low


def dot(a, b):
    return jnp.dot(a, b, preferred_element_type=F32)


def lanes_to_sublanes(row):
    n = row.shape[1]
    same = lax.broadcasted_iota(jnp.int32, (n, n), 0) == lax.broadcasted_iota(jnp.int32, (n, n), 1)
    return jnp.sum(jnp.where(same, row, jnp.zeros_like(row)), axis=1, keepdims=True)


def sublanes_to_lanes(column):
    n = column.shape[0]
    same = lax.broadcasted_iota(jnp.int32, (n, n), 0) == lax.broadcasted_iota(jnp.int32, (n, n), 1)
    return jnp.sum(jnp.where(same, column, jnp.zeros_like(column)), axis=0, keepdims=True)


def folded(x):
    total = x[:, :128]
    for start in range(128, x.shape[1], 128):
        total = total + x[:, start : start + 128]
    return total


def cg_coefficients(m):
    m0, m1, m2, m3, m4, m5 = m
    a0 = m0 / m1
    rr1 = m0 - 2.0 * a0 * m1 + a0 * a0 * m2
    b0 = rr1 / m0
    p0, p1 = 1.0 + b0, -a0
    a1 = rr1 / (p0 * p0 * m1 + 2.0 * p0 * p1 * m2 + p1 * p1 * m3)
    r0, r1, r2 = 1.0, -a0 - a1 * p0, -a1 * p1
    rr2 = m0 + r1 * r1 * m2 + r2 * r2 * m4 + 2.0 * (r1 * m1 + r2 * m2 + r1 * r2 * m3)
    b1 = rr2 / rr1
    q0, q1, q2 = r0 + b1 * p0, r1 + b1 * p1, r2
    curv = q0 * q0 * m1 + q1 * q1 * m3 + q2 * q2 * m5
    curv = curv + 2.0 * (q0 * q1 * m2 + q0 * q2 * m3 + q1 * q2 * m4)
    a2 = rr2 / curv
    return a0 + a1 * p0 + a2 * q0, a1 * p1 + a2 * q1, a2 * q2


def kernel(
    frames, slabs, regions,
    labels_ref, cond_ref, source_ref, recv_hbm, obs_hbm,
    out_ref, misfit_ref,
    lab, src, recv_ref, obs_ref, h, v0, v1, v2, diag, kxo, kxm, kyo, kym, kz,
    czb, qs, up, tall, gat, hot_y, msg, got1, got2, pmsg, pgot, dmsg, dgot, wq, wg, cmsg, cgot, uq, uf,
    load_sem, h_send, h_recv, q_send, q_recv, ar_send, ar_recv, p_send, p_recv, y_send, y_recv, known,
):
    nx, ny = lab.shape[1], lab.shape[2]
    nxc, nyc = nx // 2, ny // 2
    recv = recv_ref.shape[1]
    quarter = nxc // frames
    chunks = nx // ROWS
    f = lax.axis_index("frame")
    s = lax.axis_index("space")

    def slab_at(by):
        return lax.rem(s + by + slabs, slabs)

    def frame_at(by):
        return lax.rem(f + by, frames)

    barrier = pltpu.get_barrier_semaphore()

    def tell(semaphore, slabs_by, others):
        for by in slabs_by:
            pl.semaphore_signal(semaphore, inc=1, device_id=(f, slab_at(by)), device_id_type=MESH)
        if others:
            for k in range(1, frames):
                pl.semaphore_signal(semaphore, inc=1, device_id=(frame_at(k), s), device_id_type=MESH)
        return len(slabs_by) + (frames - 1 if others else 0)

    reach = slabs // 16
    quarters = [slabs // 4, slabs // 2, slabs - slabs // 4]
    near = [by for k in range(1, reach + 1) for by in (k, -k)]
    greeted = tell(barrier, near + quarters, True)

    load_labels = pltpu.make_async_copy(labels_ref, lab, load_sem.at[0])
    load_source = pltpu.make_async_copy(source_ref.at[0, :, 0], src, load_sem.at[1])
    load_labels.start()
    load_source.start()
    load_recv = pltpu.make_async_copy(recv_hbm.at[:, 0], recv_ref, load_sem.at[2])
    load_obs = pltpu.make_async_copy(obs_hbm, obs_ref, load_sem.at[3])
    load_recv.start()
    load_obs.start()

    load_labels.wait()

    def convert(i, carry):
        p, r = i // chunks, i % chunks
        here = lab[p, pl.ds(pl.multiple_of(r * ROWS, ROWS), ROWS), :]
        value = jnp.full((ROWS, ny), 0.5 * cond_ref[0], F32)
        for region in range(1, regions):
            value = jnp.where(here == region, 0.5 * cond_ref[region], value)
        h[p + 2, pl.ds(pl.multiple_of(PAD + r * ROWS, ROWS), ROWS), :] = value
        return carry

    lax.fori_loop(0, 2 * chunks, convert, 0, unroll=chunks)
    load_source.wait()

    pl.semaphore_wait(barrier, greeted)
    heard = tell(known.at[0], [reach, -reach], True)

    def remote(src_ref, dst_ref, sems, index, device):
        return pltpu.make_async_remote_copy(
            src_ref=src_ref, dst_ref=dst_ref, send_sem=sems[0].at[index], recv_sem=sems[1].at[index],
            device_id=device, device_id_type=MESH,
        )

    def send(*args):
        copy = remote(*args)
        copy.start()
        return copy

    def plane(p):
        return h.at[p, pl.ds(PAD, nx), :]

    def strip(p):
        rows = nx // frames
        return h.at[p, pl.ds(pl.multiple_of(PAD + f * rows, ROWS), rows), :]

    copy_cz = send(src.at[0], czb, (q_send, q_recv), 0, (f, slab_at(1)))
    h_sems = (h_send, h_recv)
    odd = lax.rem(s, 2) == 1
    copy_strip = remote(strip(2), strip(6), h_sems, 4, (f, slab_at(-2)))
    copies_strip = [remote(strip(6), strip(6), h_sems, 5 + k, (frame_at(k), s)) for k in range(1, frames)]
    copy_relay = remote(plane(4), plane(6), h_sems, 5, (f, slab_at(-1)))
    pl.when(odd)(copy_strip.start)
    copy_h1 = send(plane(3), plane(1), h_sems, 0, (f, slab_at(1)))
    copy_h4 = send(plane(2), plane(4), h_sems, 1, (f, slab_at(-1)))

    row_c = lax.broadcasted_iota(jnp.int32, (nxc, nyc), 0)
    lane_c = lax.broadcasted_iota(jnp.int32, (nxc, nyc), 1)
    along_x, along_y = src[1], src[2]
    total = src[0] + along_x - jnp.where(row_c > 0, pltpu.roll(along_x, 1, 0), 0.0)
    total = total + along_y - jnp.where(lane_c > 0, pltpu.roll(along_y, 1, 1), 0.0)
    copy_cz.wait_recv()
    qs[1] = total - jnp.where(s > 0, czb[...], 0.0)
    q_sems = (q_send, q_recv)
    copies_q = [
        send(qs.at[1], qs.at[0], q_sems, 1, (f, slab_at(1))),
        send(qs.at[1], qs.at[2], q_sems, 2, (f, slab_at(-1))),
    ]
    copy_q3 = remote(qs.at[1], qs.at[3], q_sems, 3, (f, slab_at(-2)))
    relay_q3 = remote(qs.at[2], qs.at[3], q_sems, 4, (f, slab_at(-1)))
    pl.when(odd)(copy_q3.start)

    copy_h0 = send(plane(2), plane(0), h_sems, 2, (f, slab_at(1)))
    copy_h5 = send(plane(3), plane(5), h_sems, 3, (f, slab_at(-1)))
    zero_rows = jnp.zeros((PAD, ny), F32)
    for field in (h, v0, v1, v2):
        for p in range(PLANES):
            field[p, 0:PAD, :] = zero_rows
            field[p, PAD + nx : PAD + nx + PAD, :] = zero_rows
    load_recv.wait()
    load_obs.wait()
    first = 2 * s - 2
    zx_row = (recv_ref[0:1, :] - first) * nx + recv_ref[1:2, :]
    zx_col = lanes_to_sublanes(zx_row)
    y_col = lanes_to_sublanes(recv_ref[2:3, :])
    own_ids = lax.broadcasted_iota(jnp.int32, (recv, 2 * nx), 1) + 2 * nx
    gat[...] = (zx_col == own_ids).astype(BF16)
    hot_y[...] = (y_col == lax.broadcasted_iota(jnp.int32, (recv, ny), 1)).astype(BF16)
    coarse_id = lax.broadcasted_iota(jnp.int32, (nyc, ny), 0)
    up[...] = (coarse_id == lax.broadcasted_iota(jnp.int32, (nyc, ny), 1) // 2).astype(BF16)
    z_in = recv_ref[0:1, :] - 2 * s
    inside = (z_in >= 0) & (z_in < 2)

    def valid(p):
        z = first + p
        return (z >= 0) & (z < 2 * slabs)

    def aligned(r):
        return pl.ds(pl.multiple_of(PAD + r * ROWS, ROWS), ROWS)

    def next_row(field, p, r, here):
        return pltpu.roll(jnp.where(sub == 0, field[p, aligned(r + 1), :], here), ROWS - 1, 0)

    def previous_row(field, p, r, here):
        return pltpu.roll(jnp.where(sub == ROWS - 1, field[p, aligned(r - 1), :], here), 1, 0)

    def prolong(c):
        z = s - 1 + c
        ok = (z >= 0) & (z < slabs)
        high, middle, low = parts_of(jnp.where(ok, qs[c], 0.0))
        fine = dot(high, up[...]) + dot(middle, up[...]) + dot(low, up[...])
        for t in range(ny // 128):
            tall[t, pl.ds(0, nxc, 2), :] = fine[:, t * 128 : t * 128 + 128]
            tall[t, pl.ds(1, nxc, 2), :] = fine[:, t * 128 : t * 128 + 128]
        for p in (2 * c, 2 * c + 1):
            if p < PLANES:
                for t in range(ny // 128):
                    v0[p, PAD : PAD + nx, t * 128 : t * 128 + 128] = tall[t]

    lane = lax.broadcasted_iota(jnp.int32, (ROWS, ny), 1)
    sub = lax.broadcasted_iota(jnp.int32, (ROWS, ny), 0)

    def zero_outside(p):
        @pl.when(jnp.logical_not(valid(p)))
        def _():
            h[p, PAD : PAD + nx, :] = jnp.zeros((nx, ny), F32)

    def vertical(e):
        keep = jnp.where(valid(e) & valid(e + 1), 1.0, 0.0).astype(F32)

        def body(r, carry):
            kz[e, pl.ds(pl.multiple_of(r * ROWS, ROWS), ROWS), :] = keep * (h[e, aligned(r), :] + h[e + 1, aligned(r), :])
            return carry

        lax.fori_loop(0, chunks, body, 0, unroll=chunks)

    def coefficients(p):
        def body(r, carry):
            at = pl.ds(pl.multiple_of(r * ROWS, ROWS), ROWS)
            here = h[p, aligned(r), :]
            x_next, x_prev = next_row(h, p, r, here), previous_row(h, p, r, here)
            y_next = jnp.where(lane < ny - 1, pltpu.roll(here, ny - 1, 1), 0.0)
            y_prev = jnp.where(lane > 0, pltpu.roll(here, 1, 1), 0.0)
            kxo[p, at, :] = here + x_next
            kxm[p, at, :] = here + x_prev
            kyo[p, at, :] = jnp.where(lane < ny - 1, here + y_next, 0.0)
            kym[p, at, :] = jnp.where(lane > 0, here + y_prev, 0.0)
            near = x_next + x_prev + y_next + y_prev
            diag[p, at, :] = 6.0 * here + near + h[p - 1, aligned(r), :] + h[p + 1, aligned(r), :]
            return carry

        lax.fori_loop(0, chunks, body, 0, unroll=chunks)

    def operate(src_v, dst_v, p, with_moments, sums):
        def body(r, carry):
            at = pl.ds(pl.multiple_of(r * ROWS, ROWS), ROWS)
            here = src_v[p, aligned(r), :]
            value = diag[p, at, :] * here
            value = value - kxo[p, at, :] * next_row(src_v, p, r, here)
            value = value - kxm[p, at, :] * previous_row(src_v, p, r, here)
            value = value - kyo[p, at, :] * pltpu.roll(here, ny - 1, 1)
            value = value - kym[p, at, :] * pltpu.roll(here, 1, 1)
            value = value - kz[p, at, :] * src_v[p + 1, aligned(r), :]
            value = value - kz[p - 1, at, :] * src_v[p - 1, aligned(r), :]
            dst_v[p, aligned(r), :] = value
            if not with_moments:
                return carry
            return (carry[0] + folded(here * value), carry[1] + folded(value * value))

        return lax.fori_loop(0, chunks, body, sums, unroll=chunks)

    def square(src_v, p, total):
        def body(r, carry):
            here = src_v[p, aligned(r), :]
            return carry + folded(here * here)

        return lax.fori_loop(0, chunks, body, total, unroll=chunks)

    def energy(field, p, total):
        def body(r, carry):
            at = pl.ds(pl.multiple_of(r * ROWS, ROWS), ROWS)
            here = field[p, aligned(r), :]
            near = kxo[p, at, :] * next_row(field, p, r, here)
            near = near + kyo[p, at, :] * pltpu.roll(here, ny - 1, 1)
            near = near + kz[p, at, :] * field[p + 1, aligned(r), :]
            return carry + folded(here * (diag[p, at, :] * here - 2.0 * near))

        return lax.fori_loop(0, chunks, body, total, unroll=chunks)

    nothing = jnp.zeros((ROWS, 128), F32)

    def krylov_own():
        m0 = square(v0, 3, square(v0, 2, nothing))
        return m0, operate(v0, v1, 3, True, operate(v0, v1, 2, True, (nothing, nothing)))

    def krylov_near():
        for p in (1, 4):
            operate(v0, v1, p, False, 0)
        m34 = operate(v1, v2, 3, True, operate(v1, v2, 2, True, (nothing, nothing)))
        return m34, energy(v2, 2, nothing)

    def krylov_far(m5):
        operate(v0, v1, 5, False, 0)
        operate(v1, v2, 4, False, 0)
        return energy(v2, 3, m5)

    def summed(*moments):
        place = lax.broadcasted_iota(jnp.int32, (1, 128), 1)
        row = jnp.zeros((1, 128), F32)
        for j, m in enumerate(moments):
            row = jnp.where(place == j, jnp.sum(jnp.sum(m, axis=0, keepdims=True), axis=1, keepdims=True), row)
        return row

    def share(source, landing, index):
        def start(i, carry):
            k = lax.rem(i + slabs // 2, slabs - 1) + 1
            pltpu.make_async_remote_copy(
                src_ref=source, dst_ref=landing.at[s], send_sem=ar_send.at[index], recv_sem=ar_recv.at[index],
                device_id=(f, slab_at(k)), device_id_type=MESH,
            ).start()
            return carry

        lax.fori_loop(0, slabs - 1, start, 0)

    def shared(landing, index):
        others = landing.at[pl.ds(0, slabs - 1)]
        whole = pltpu.make_async_remote_copy(
            src_ref=others, dst_ref=others, send_sem=ar_send.at[index], recv_sem=ar_recv.at[index],
            device_id=(f, slab_at(1)), device_id_type=MESH,
        )
        whole.wait_send()
        whole.wait_recv()

    def moments_of(landing):
        total = jnp.sum(landing[...], axis=0)
        return [total[:, j : j + 1] for j in range(6)]

    @pl.when(odd)
    def _():
        copy_strip.wait_recv()
        for copy in copies_strip:
            copy.start()

    copy_h1.wait_recv()
    copy_h4.wait_recv()
    zero_outside(1)
    zero_outside(4)
    pl.when(odd)(copy_relay.start)
    for e in (1, 2, 3):
        vertical(e)
    for p in (2, 3):
        coefficients(p)
    for copy in copies_q:
        copy.wait_recv()
    pl.when(odd)(relay_q3.start)
    for c in range(3):
        prolong(c)
    m0, m12 = krylov_own()
    pl.semaphore_wait(known.at[0], heard)
    heard = tell(known.at[1], quarters, False)
    copy_h0.wait_recv()
    copy_h5.wait_recv()
    zero_outside(0)
    zero_outside(5)
    vertical(0)
    vertical(4)
    coefficients(1)
    coefficients(4)
    m34, m5 = krylov_near()

    @pl.when(odd)
    def _():
        copy_q3.wait_recv()
        for copy in copies_strip:
            copy.wait()

    @pl.when(jnp.logical_not(odd))
    def _():
        relay_q3.wait_recv()
        copy_relay.wait_recv()

    prolong(3)
    zero_outside(6)
    vertical(5)
    coefficients(5)
    m5 = krylov_far(m5)
    moments = summed(m0, *m12, *m34, m5)
    msg[0] = moments
    got1[s] = moments
    pl.semaphore_wait(known.at[1], heard)
    share(msg.at[0], got1, 0)

    for j, field in enumerate((v0, v1, v2)):
        whole = jnp.concatenate([field[2, PAD : PAD + nx, :], field[3, PAD : PAD + nx, :]], axis=0)
        rows = sum(dot(gat[...], part) for part in parts_of(whole))
        column = jnp.sum(rows * hot_y[...].astype(F32), axis=1, keepdims=True)
        pmsg[j] = sublanes_to_lanes(column)
    p_sems = (p_send, p_recv)
    copies_p = [
        send(pmsg, pgot.at[0], p_sems, 0, (f, slab_at(1))),
        send(pmsg, pgot.at[1], p_sems, 1, (f, slab_at(-1))),
        send(pmsg, pgot.at[2], p_sems, 2, (f, slab_at(-2))),
    ]
    shared(got1, 0)
    c0, c1, c2 = cg_coefficients(moments_of(got1))
    observed = obs_ref[...]

    def misfit(values):
        return c0 * values[0] + c1 * values[1] + c2 * values[2] - observed

    mine = jnp.where(inside, misfit([pmsg[j] for j in range(3)]), 0.0)
    dmsg[...] = mine
    dgot[s] = mine
    share(dmsg, dgot, 1)
    for copy in copies_p:
        copy.wait_recv()
    d = misfit([pmsg[j] + pgot[0, j] + pgot[1, j] + pgot[2, j] for j in range(3)])

    d_parts = parts_of(d)
    for p in range(PLANES):
        hit = zx_row == lax.broadcasted_iota(jnp.int32, (nx, recv), 0) + p * nx
        value = sum(dot(jnp.where(hit, part.astype(F32), 0.0).astype(BF16), hot_y[...]) for part in d_parts)
        v0[p, PAD : PAD + nx, :] = jnp.where(valid(p), value, 0.0)
    m0, m12 = krylov_own()
    m34, m5 = krylov_near()
    moments = summed(m0, *m12, *m34, krylov_far(m5))
    msg[1] = moments
    got2[s] = moments
    share(msg.at[1], got2, 2)
    down = (((1,), (1,)), ((), ()))
    for j, field in enumerate((v0, v1, v2)):
        for t in range(ny // 128):
            at = slice(t * 128, t * 128 + 128)
            tall[t] = field[2, PAD : PAD + nx, at] + field[3, PAD : PAD + nx, at]
        pairs = jnp.concatenate(
            [tall[t, pl.ds(0, nxc, 2), :] + tall[t, pl.ds(1, nxc, 2), :] for t in range(ny // 128)], axis=1
        )
        coarse = sum(lax.dot_general(part, up[...], down, preferred_element_type=F32) for part in parts_of(pairs))
        for g in range(frames):
            wq[g, j] = coarse[g * quarter : (g + 1) * quarter]
    y_sems = (y_send, y_recv)
    wg[0, f] = wq[f]
    copies_w = [send(wq.at[f], wg.at[1, f], y_sems, 0, (f, slab_at(-1)))]
    for k in range(1, frames):
        to = frame_at(k)
        copies_w.append(send(wq.at[to], wg.at[1, f], y_sems, k, (to, slab_at(-1))))
        copies_w.append(send(wq.at[to], wg.at[0, f], y_sems, frames + k, (to, s)))
    shared(got2, 2)
    place = lax.broadcasted_iota(jnp.int32, (1, 128), 1)
    c_row = jnp.zeros((1, 128), F32)
    for j, c in enumerate(cg_coefficients(moments_of(got2))):
        c_row = jnp.where(place == j, c, c_row)
    cmsg[...] = c_row
    cgot[f] = c_row
    copies_c = [send(cmsg, cgot.at[f], y_sems, 2 * frames + k, (frame_at(k), s)) for k in range(1, frames)]

    for copy in copies_w:
        copy.wait_recv()
    for copy in copies_c:
        copy.wait_recv()
    inverse = smoothing_inverse(frames)
    for side in range(2):
        w = [sum(cgot[k][:, j : j + 1] * wg[side, k, j] for j in range(3)) for k in range(frames)]
        for g in range(frames):
            uq[g, side] = sum(float(inverse[g, k]) * w[k] for k in range(frames))
    uf[f] = uq[f]
    copies_u = [send(uq.at[frame_at(k)], uf.at[f], y_sems, 3 * frames + k, (frame_at(k), s)) for k in range(1, frames)]
    shared(dgot, 1)
    misfit_ref[...] = jnp.sum(dgot[...], axis=0)
    for copy in copies_u:
        copy.wait_recv()
    u = jnp.concatenate([uf[g, 0] for g in range(frames)], axis=0)
    above = jnp.concatenate([uf[g, 1] for g in range(frames)], axis=0)
    out_ref[0] = u - jnp.where(s < slabs - 1, above, 0.0)
    out_ref[1] = u - jnp.where(row_c < nxc - 1, pltpu.roll(u, nxc - 1, 0), 0.0)
    out_ref[2] = u - jnp.where(lane_c < nyc - 1, pltpu.roll(u, nyc - 1, 1), 0.0)

    @pl.when(odd)
    def _():
        for copy in [copy_strip, copy_relay, copy_q3, relay_q3]:
            copy.wait_send()

    for copy in [copy_cz, copy_h0, copy_h1, copy_h4, copy_h5, *copies_q, *copies_p, *copies_w, *copies_c, *copies_u]:
        copy.wait_send()


def shards(frames, slabs, labels, region_conductivity, source, receivers, observed):
    _, nx, ny = labels.shape
    nxc, nyc = nx // 2, ny // 2
    recv = receivers.shape[2]
    quarter = nxc // frames
    vmem = pl.BlockSpec(memory_space=pltpu.VMEM)
    hbm = pl.BlockSpec(memory_space=pltpu.HBM)
    plane = (PLANES, nx, ny)
    padded = (PLANES, nx + 2 * PAD, ny)
    scratch = [
        pltpu.VMEM((2, nx, ny), jnp.int32),
        pltpu.VMEM((3, nxc, nyc), F32),
        pltpu.VMEM((3, recv), jnp.int32),
        pltpu.VMEM((1, recv), F32),
        *[pltpu.VMEM(padded, F32) for _ in range(4)],
        *[pltpu.VMEM(plane, F32) for _ in range(6)],
        pltpu.VMEM((nxc, nyc), F32),
        pltpu.VMEM((4, nxc, nyc), F32),
        pltpu.VMEM((nyc, ny), BF16),
        pltpu.VMEM((ny // 128, nx, 128), F32),
        pltpu.VMEM((recv, 2 * nx), BF16),
        pltpu.VMEM((recv, ny), BF16),
        pltpu.VMEM((2, 1, 128), F32),
        pltpu.VMEM((slabs, 1, 128), F32),
        pltpu.VMEM((slabs, 1, 128), F32),
        pltpu.VMEM((3, 1, recv), F32),
        pltpu.VMEM((3, 3, 1, recv), F32),
        pltpu.VMEM((1, recv), F32),
        pltpu.VMEM((slabs, 1, recv), F32),
        pltpu.VMEM((frames, 3, quarter, nyc), F32),
        pltpu.VMEM((2, frames, 3, quarter, nyc), F32),
        pltpu.VMEM((1, 128), F32),
        pltpu.VMEM((frames, 1, 128), F32),
        pltpu.VMEM((frames, 2, quarter, nyc), F32),
        pltpu.VMEM((frames, 2, quarter, nyc), F32),
        pltpu.SemaphoreType.DMA((4,)),
        *[pltpu.SemaphoreType.DMA((5 + frames,)) for _ in range(2)],
        *[pltpu.SemaphoreType.DMA((5,)) for _ in range(2)],
        *[pltpu.SemaphoreType.DMA((3,)) for _ in range(2)],
        *[pltpu.SemaphoreType.DMA((3,)) for _ in range(2)],
        *[pltpu.SemaphoreType.DMA((4 * frames,)) for _ in range(2)],
        pltpu.SemaphoreType.REGULAR((2,)),
    ]
    out, misfit = pl.pallas_call(
        functools.partial(kernel, frames, slabs, region_conductivity.shape[0]),
        out_shape=(jax.ShapeDtypeStruct((3, nxc, nyc), F32), jax.ShapeDtypeStruct((1, recv), F32)),
        in_specs=[hbm, pl.BlockSpec(memory_space=pltpu.SMEM), hbm, hbm, hbm],
        out_specs=(vmem, vmem),
        scratch_shapes=scratch,
        compiler_params=pltpu.CompilerParams(
            collective_id=0, has_side_effects=True, vmem_limit_bytes=64 * 1024 * 1024
        ),
    )(labels, region_conductivity, source, jnp.transpose(receivers, (1, 0, 2)), observed)
    return out.reshape(1, 3, 1, nxc, nyc), misfit


def solution(mesh):
    in_specs = (
        P("space", None, None),
        P(),
        P("frame", None, "space", None, None),
        P("frame", None, None),
        P("frame", None),
    )
    out_specs = (P("frame", None, "space", None, None), P("frame", None))
    body = functools.partial(shards, mesh.shape["frame"], mesh.shape["space"])
    return jax.shard_map(body, mesh=mesh, in_specs=in_specs, out_specs=out_specs, check_vma=False)
```

```python
import functools

import jax
import jax.numpy as jnp
import numpy as np
from jax import lax
from jax.experimental import pallas as pl
from jax.experimental.pallas import tpu as pltpu
from jax.sharding import PartitionSpec as P

SMOOTHING = 4.0
PAD = 8
ROWS = 8
PLANES = 7
MESH = pl.DeviceIdType.MESH
F32 = jnp.float32
BF16 = jnp.bfloat16


def smoothing_inverse(frames):
    matrix = np.zeros((frames, frames))
    for f in range(frames):
        near = [g for g in (f - 1, f + 1) if 0 <= g < frames]
        matrix[f, f] = 1.0 + SMOOTHING * len(near)
        for g in near:
            matrix[f, g] = -SMOOTHING
    return np.linalg.inv(matrix)


def parts_of(x):
    high = x.astype(BF16)
    rest = x - high.astype(F32)
    middle = rest.astype(BF16)
    low = (rest - middle.astype(F32)).astype(BF16)
    return high, middle, low


def dot(a, b):
    return jnp.dot(a, b, preferred_element_type=F32)


def lanes_to_sublanes(row):
    n = row.shape[1]
    same = lax.broadcasted_iota(jnp.int32, (n, n), 0) == lax.broadcasted_iota(jnp.int32, (n, n), 1)
    return jnp.sum(jnp.where(same, row, jnp.zeros_like(row)), axis=1, keepdims=True)


def sublanes_to_lanes(column):
    n = column.shape[0]
    same = lax.broadcasted_iota(jnp.int32, (n, n), 0) == lax.broadcasted_iota(jnp.int32, (n, n), 1)
    return jnp.sum(jnp.where(same, column, jnp.zeros_like(column)), axis=0, keepdims=True)


def folded(x):
    total = x[:, :128]
    for start in range(128, x.shape[1], 128):
        total = total + x[:, start : start + 128]
    return total


def cg_coefficients(m):
    m0, m1, m2, m3, m4, m5 = m
    a0 = m0 / m1
    rr1 = m0 - 2.0 * a0 * m1 + a0 * a0 * m2
    b0 = rr1 / m0
    p0, p1 = 1.0 + b0, -a0
    a1 = rr1 / (p0 * p0 * m1 + 2.0 * p0 * p1 * m2 + p1 * p1 * m3)
    r0, r1, r2 = 1.0, -a0 - a1 * p0, -a1 * p1
    rr2 = m0 + r1 * r1 * m2 + r2 * r2 * m4 + 2.0 * (r1 * m1 + r2 * m2 + r1 * r2 * m3)
    b1 = rr2 / rr1
    q0, q1, q2 = r0 + b1 * p0, r1 + b1 * p1, r2
    curv = q0 * q0 * m1 + q1 * q1 * m3 + q2 * q2 * m5
    curv = curv + 2.0 * (q0 * q1 * m2 + q0 * q2 * m3 + q1 * q2 * m4)
    a2 = rr2 / curv
    return a0 + a1 * p0 + a2 * q0, a1 * p1 + a2 * q1, a2 * q2


def kernel(
    frames, slabs, regions,
    labels_ref, cond_ref, source_ref, recv_hbm, obs_hbm,
    out_ref, misfit_ref,
    lab, src, recv_ref, obs_ref, h, v0, v1, v2, diag, kxo, kxm, kyo, kym, kz,
    czb, qs, up, tall, gat, hot_y, msg, got1, got2, pmsg, pgot, dmsg, dgot, wq, wg, cmsg, cgot, uq, uf,
    load_sem, h_send, h_recv, g_send, g_recv, q_send, q_recv, ar_send, ar_recv, p_send, p_recv, y_send, y_recv, known,
):
    nx, ny = lab.shape[1], lab.shape[2]
    nxc, nyc = nx // 2, ny // 2
    recv = recv_ref.shape[1]
    quarter = nxc // frames
    chunks = nx // ROWS
    f = lax.axis_index("frame")
    s = lax.axis_index("space")

    def slab_at(by):
        return lax.rem(s + by + slabs, slabs)

    def frame_at(by):
        return lax.rem(f + by, frames)

    barrier = pltpu.get_barrier_semaphore()

    def tell(semaphore, slabs_by, others):
        for by in slabs_by:
            pl.semaphore_signal(semaphore, inc=1, device_id=(f, slab_at(by)), device_id_type=MESH)
        if others:
            for k in range(1, frames):
                pl.semaphore_signal(semaphore, inc=1, device_id=(frame_at(k), s), device_id_type=MESH)
        return len(slabs_by) + (frames - 1 if others else 0)

    reach = slabs // 16
    quarters = [slabs // 4, slabs // 2, slabs - slabs // 4]
    near = [by for k in range(1, reach + 1) for by in (k, -k)]
    greeted = tell(barrier, near + quarters, True)

    load_labels = pltpu.make_async_copy(labels_ref, lab, load_sem.at[0])
    load_source = pltpu.make_async_copy(source_ref.at[0, :, 0], src, load_sem.at[1])
    load_labels.start()
    load_source.start()
    load_recv = pltpu.make_async_copy(recv_hbm.at[:, 0], recv_ref, load_sem.at[2])
    load_obs = pltpu.make_async_copy(obs_hbm, obs_ref, load_sem.at[3])
    load_recv.start()
    load_obs.start()

    load_labels.wait()

    def convert(i, carry):
        p, r = i // chunks, i % chunks
        here = lab[p, pl.ds(pl.multiple_of(r * ROWS, ROWS), ROWS), :]
        value = jnp.full((ROWS, ny), 0.5 * cond_ref[0], F32)
        for region in range(1, regions):
            value = jnp.where(here == region, 0.5 * cond_ref[region], value)
        h[p + 2, pl.ds(pl.multiple_of(PAD + r * ROWS, ROWS), ROWS), :] = value
        return carry

    lax.fori_loop(0, 2 * chunks, convert, 0, unroll=chunks)
    load_source.wait()

    pl.semaphore_wait(barrier, greeted)
    heard = tell(known.at[0], [reach, -reach], True)

    def remote(src_ref, dst_ref, sems, index, device):
        return pltpu.make_async_remote_copy(
            src_ref=src_ref, dst_ref=dst_ref, send_sem=sems[0].at[index], recv_sem=sems[1].at[index],
            device_id=device, device_id_type=MESH,
        )

    def send(*args):
        copy = remote(*args)
        copy.start()
        return copy

    def plane(p):
        return h.at[p, pl.ds(PAD, nx), :]

    def strip(p):
        rows = nx // frames
        return h.at[p, pl.ds(pl.multiple_of(PAD + f * rows, ROWS), rows), :]

    def half(p, which):
        return h.at[p, pl.ds(PAD + which * (nx // 2), nx // 2), :]

    def thin(p):
        rows = nx // 2 // frames
        return h.at[p, pl.ds(pl.multiple_of(PAD + nx // 2 + f * rows, ROWS), rows), :]

    copy_cz = send(src.at[0], czb, (q_send, q_recv), 0, (f, slab_at(1)))
    h_sems = (h_send, h_recv)
    odd = lax.rem(s, 2) == 1
    copy_strip = remote(strip(2), strip(6), h_sems, 4, (f, slab_at(-2)))
    copies_strip = [remote(strip(6), strip(6), h_sems, 5 + k, (frame_at(k), s)) for k in range(1, frames)]
    copy_relay = remote(plane(4), plane(6), h_sems, 5, (f, slab_at(-1)))
    even = jnp.logical_not(odd)
    g_sems = (g_send, g_recv)
    copy_h0b = remote(half(2, 1), half(0, 1), g_sems, 0, (f, slab_at(1)))
    copy_h5b = remote(half(3, 1), half(5, 1), g_sems, 0, (f, slab_at(-1)))
    copy_up = remote(thin(2), thin(0), g_sems, 1, (f, slab_at(1)))
    copy_down = remote(thin(3), thin(5), g_sems, 1, (f, slab_at(-1)))
    copies_up = [remote(thin(0), thin(0), g_sems, 1 + k, (frame_at(k), s)) for k in range(1, frames)]
    copies_down = [remote(thin(5), thin(5), g_sems, 1 + k, (frame_at(k), s)) for k in range(1, frames)]

    @pl.when(odd)
    def _():
        copy_up.start()
        copy_strip.start()

    pl.when(even)(copy_down.start)
    copy_h1 = send(plane(3), plane(1), h_sems, 0, (f, slab_at(1)))
    copy_h4 = send(plane(2), plane(4), h_sems, 1, (f, slab_at(-1)))

    row_c = lax.broadcasted_iota(jnp.int32, (nxc, nyc), 0)
    lane_c = lax.broadcasted_iota(jnp.int32, (nxc, nyc), 1)
    along_x, along_y = src[1], src[2]
    total = src[0] + along_x - jnp.where(row_c > 0, pltpu.roll(along_x, 1, 0), 0.0)
    total = total + along_y - jnp.where(lane_c > 0, pltpu.roll(along_y, 1, 1), 0.0)
    copy_cz.wait_recv()
    qs[1] = total - jnp.where(s > 0, czb[...], 0.0)
    q_sems = (q_send, q_recv)
    copies_q = [
        send(qs.at[1], qs.at[0], q_sems, 1, (f, slab_at(1))),
        send(qs.at[1], qs.at[2], q_sems, 2, (f, slab_at(-1))),
    ]
    copy_q3 = remote(qs.at[1], qs.at[3], q_sems, 3, (f, slab_at(-2)))
    relay_q3 = remote(qs.at[2], qs.at[3], q_sems, 4, (f, slab_at(-1)))
    pl.when(odd)(copy_q3.start)

    copy_h0 = send(half(2, 0), half(0, 0), h_sems, 2, (f, slab_at(1)))
    copy_h5 = send(half(3, 0), half(5, 0), h_sems, 3, (f, slab_at(-1)))
    pl.when(even)(copy_h0b.start)
    pl.when(odd)(copy_h5b.start)
    zero_rows = jnp.zeros((PAD, ny), F32)
    for field in (h, v0, v1, v2):
        for p in range(PLANES):
            field[p, 0:PAD, :] = zero_rows
            field[p, PAD + nx : PAD + nx + PAD, :] = zero_rows
    load_recv.wait()
    load_obs.wait()
    first = 2 * s - 2
    zx_row = (recv_ref[0:1, :] - first) * nx + recv_ref[1:2, :]
    zx_col = lanes_to_sublanes(zx_row)
    y_col = lanes_to_sublanes(recv_ref[2:3, :])
    own_ids = lax.broadcasted_iota(jnp.int32, (recv, 2 * nx), 1) + 2 * nx
    gat[...] = (zx_col == own_ids).astype(BF16)
    hot_y[...] = (y_col == lax.broadcasted_iota(jnp.int32, (recv, ny), 1)).astype(BF16)
    coarse_id = lax.broadcasted_iota(jnp.int32, (nyc, ny), 0)
    up[...] = (coarse_id == lax.broadcasted_iota(jnp.int32, (nyc, ny), 1) // 2).astype(BF16)
    z_in = recv_ref[0:1, :] - 2 * s
    inside = (z_in >= 0) & (z_in < 2)

    def valid(p):
        z = first + p
        return (z >= 0) & (z < 2 * slabs)

    def aligned(r):
        return pl.ds(pl.multiple_of(PAD + r * ROWS, ROWS), ROWS)

    def next_row(field, p, r, here):
        return pltpu.roll(jnp.where(sub == 0, field[p, aligned(r + 1), :], here), ROWS - 1, 0)

    def previous_row(field, p, r, here):
        return pltpu.roll(jnp.where(sub == ROWS - 1, field[p, aligned(r - 1), :], here), 1, 0)

    def prolong(c):
        z = s - 1 + c
        ok = (z >= 0) & (z < slabs)
        high, middle, low = parts_of(jnp.where(ok, qs[c], 0.0))
        fine = dot(high, up[...]) + dot(middle, up[...]) + dot(low, up[...])
        for t in range(ny // 128):
            tall[t, pl.ds(0, nxc, 2), :] = fine[:, t * 128 : t * 128 + 128]
            tall[t, pl.ds(1, nxc, 2), :] = fine[:, t * 128 : t * 128 + 128]
        for p in (2 * c, 2 * c + 1):
            if p < PLANES:
                for t in range(ny // 128):
                    v0[p, PAD : PAD + nx, t * 128 : t * 128 + 128] = tall[t]

    lane = lax.broadcasted_iota(jnp.int32, (ROWS, ny), 1)
    sub = lax.broadcasted_iota(jnp.int32, (ROWS, ny), 0)

    def zero_outside(p):
        @pl.when(jnp.logical_not(valid(p)))
        def _():
            h[p, PAD : PAD + nx, :] = jnp.zeros((nx, ny), F32)

    def vertical(e):
        keep = jnp.where(valid(e) & valid(e + 1), 1.0, 0.0).astype(F32)

        def body(r, carry):
            kz[e, pl.ds(pl.multiple_of(r * ROWS, ROWS), ROWS), :] = keep * (h[e, aligned(r), :] + h[e + 1, aligned(r), :])
            return carry

        lax.fori_loop(0, chunks, body, 0, unroll=chunks)

    def coefficients(p):
        def body(r, carry):
            at = pl.ds(pl.multiple_of(r * ROWS, ROWS), ROWS)
            here = h[p, aligned(r), :]
            x_next, x_prev = next_row(h, p, r, here), previous_row(h, p, r, here)
            y_next = jnp.where(lane < ny - 1, pltpu.roll(here, ny - 1, 1), 0.0)
            y_prev = jnp.where(lane > 0, pltpu.roll(here, 1, 1), 0.0)
            kxo[p, at, :] = here + x_next
            kxm[p, at, :] = here + x_prev
            kyo[p, at, :] = jnp.where(lane < ny - 1, here + y_next, 0.0)
            kym[p, at, :] = jnp.where(lane > 0, here + y_prev, 0.0)
            near = x_next + x_prev + y_next + y_prev
            diag[p, at, :] = 6.0 * here + near + h[p - 1, aligned(r), :] + h[p + 1, aligned(r), :]
            return carry

        lax.fori_loop(0, chunks, body, 0, unroll=chunks)

    def operate(src_v, dst_v, p, with_moments, sums):
        def body(r, carry):
            at = pl.ds(pl.multiple_of(r * ROWS, ROWS), ROWS)
            here = src_v[p, aligned(r), :]
            value = diag[p, at, :] * here
            value = value - kxo[p, at, :] * next_row(src_v, p, r, here)
            value = value - kxm[p, at, :] * previous_row(src_v, p, r, here)
            value = value - kyo[p, at, :] * pltpu.roll(here, ny - 1, 1)
            value = value - kym[p, at, :] * pltpu.roll(here, 1, 1)
            value = value - kz[p, at, :] * src_v[p + 1, aligned(r), :]
            value = value - kz[p - 1, at, :] * src_v[p - 1, aligned(r), :]
            dst_v[p, aligned(r), :] = value
            if not with_moments:
                return carry
            return (carry[0] + folded(here * value), carry[1] + folded(value * value))

        return lax.fori_loop(0, chunks, body, sums, unroll=chunks)

    def square(src_v, p, total):
        def body(r, carry):
            here = src_v[p, aligned(r), :]
            return carry + folded(here * here)

        return lax.fori_loop(0, chunks, body, total, unroll=chunks)

    def energy(field, p, total):
        def body(r, carry):
            at = pl.ds(pl.multiple_of(r * ROWS, ROWS), ROWS)
            here = field[p, aligned(r), :]
            near = kxo[p, at, :] * next_row(field, p, r, here)
            near = near + kyo[p, at, :] * pltpu.roll(here, ny - 1, 1)
            near = near + kz[p, at, :] * field[p + 1, aligned(r), :]
            return carry + folded(here * (diag[p, at, :] * here - 2.0 * near))

        return lax.fori_loop(0, chunks, body, total, unroll=chunks)

    nothing = jnp.zeros((ROWS, 128), F32)

    def krylov_own():
        m0 = square(v0, 3, square(v0, 2, nothing))
        return m0, operate(v0, v1, 3, True, operate(v0, v1, 2, True, (nothing, nothing)))

    def krylov_near():
        for p in (1, 4):
            operate(v0, v1, p, False, 0)
        m34 = operate(v1, v2, 3, True, operate(v1, v2, 2, True, (nothing, nothing)))
        return m34, energy(v2, 2, nothing)

    def krylov_far(m5):
        operate(v0, v1, 5, False, 0)
        operate(v1, v2, 4, False, 0)
        return energy(v2, 3, m5)

    def summed(*moments):
        place = lax.broadcasted_iota(jnp.int32, (1, 128), 1)
        row = jnp.zeros((1, 128), F32)
        for j, m in enumerate(moments):
            row = jnp.where(place == j, jnp.sum(jnp.sum(m, axis=0, keepdims=True), axis=1, keepdims=True), row)
        return row

    def share(source, landing, index):
        def start(i, carry):
            k = lax.rem(i + slabs // 2, slabs - 1) + 1
            pltpu.make_async_remote_copy(
                src_ref=source, dst_ref=landing.at[s], send_sem=ar_send.at[index], recv_sem=ar_recv.at[index],
                device_id=(f, slab_at(k)), device_id_type=MESH,
            ).start()
            return carry

        lax.fori_loop(0, slabs - 1, start, 0)

    def shared(landing, index):
        others = landing.at[pl.ds(0, slabs - 1)]
        whole = pltpu.make_async_remote_copy(
            src_ref=others, dst_ref=others, send_sem=ar_send.at[index], recv_sem=ar_recv.at[index],
            device_id=(f, slab_at(1)), device_id_type=MESH,
        )
        whole.wait_send()
        whole.wait_recv()

    def moments_of(landing):
        total = jnp.sum(landing[...], axis=0)
        return [total[:, j : j + 1] for j in range(6)]

    @pl.when(odd)
    def _():
        copy_down.wait_recv()
        for copy in copies_down:
            copy.start()
        copy_strip.wait_recv()
        for copy in copies_strip:
            copy.start()

    @pl.when(even)
    def _():
        copy_up.wait_recv()
        for copy in copies_up:
            copy.start()

    copy_h1.wait_recv()
    copy_h4.wait_recv()
    zero_outside(1)
    zero_outside(4)
    pl.when(odd)(copy_relay.start)
    for e in (1, 2, 3):
        vertical(e)
    for p in (2, 3):
        coefficients(p)
    pl.semaphore_wait(known.at[0], heard)
    heard = tell(known.at[1], quarters, False)
    for copy in copies_q:
        copy.wait_recv()
    pl.when(odd)(relay_q3.start)
    for c in range(3):
        prolong(c)
    m0, m12 = krylov_own()
    copy_h0.wait_recv()
    copy_h5.wait_recv()

    @pl.when(odd)
    def _():
        copy_h0b.wait_recv()
        for copy in copies_down:
            copy.wait()

    @pl.when(even)
    def _():
        copy_h5b.wait_recv()
        for copy in copies_up:
            copy.wait()

    zero_outside(0)
    zero_outside(5)
    vertical(0)
    vertical(4)
    coefficients(1)
    coefficients(4)
    m34, m5 = krylov_near()

    @pl.when(odd)
    def _():
        copy_q3.wait_recv()
        for copy in copies_strip:
            copy.wait()

    @pl.when(jnp.logical_not(odd))
    def _():
        relay_q3.wait_recv()
        copy_relay.wait_recv()

    prolong(3)
    zero_outside(6)
    vertical(5)
    coefficients(5)
    m5 = krylov_far(m5)
    moments = summed(m0, *m12, *m34, m5)
    msg[0] = moments
    got1[s] = moments
    pl.semaphore_wait(known.at[1], heard)
    share(msg.at[0], got1, 0)

    for j, field in enumerate((v0, v1, v2)):
        whole = jnp.concatenate([field[2, PAD : PAD + nx, :], field[3, PAD : PAD + nx, :]], axis=0)
        rows = sum(dot(gat[...], part) for part in parts_of(whole))
        column = jnp.sum(rows * hot_y[...].astype(F32), axis=1, keepdims=True)
        pmsg[j] = sublanes_to_lanes(column)
    p_sems = (p_send, p_recv)
    copies_p = [
        send(pmsg, pgot.at[0], p_sems, 0, (f, slab_at(1))),
        send(pmsg, pgot.at[1], p_sems, 1, (f, slab_at(-1))),
        send(pmsg, pgot.at[2], p_sems, 2, (f, slab_at(-2))),
    ]
    shared(got1, 0)
    c0, c1, c2 = cg_coefficients(moments_of(got1))
    observed = obs_ref[...]

    def misfit(values):
        return c0 * values[0] + c1 * values[1] + c2 * values[2] - observed

    mine = jnp.where(inside, misfit([pmsg[j] for j in range(3)]), 0.0)
    dmsg[...] = mine
    dgot[s] = mine
    for copy in copies_p:
        copy.wait_recv()
    d = misfit([pmsg[j] + pgot[0, j] + pgot[1, j] + pgot[2, j] for j in range(3)])

    d_parts = parts_of(d)
    for p in range(PLANES):
        hit = zx_row == lax.broadcasted_iota(jnp.int32, (nx, recv), 0) + p * nx
        value = sum(dot(jnp.where(hit, part.astype(F32), 0.0).astype(BF16), hot_y[...]) for part in d_parts)
        v0[p, PAD : PAD + nx, :] = jnp.where(valid(p), value, 0.0)
    m0, m12 = krylov_own()
    m34, m5 = krylov_near()
    moments = summed(m0, *m12, *m34, krylov_far(m5))
    msg[1] = moments
    got2[s] = moments
    share(msg.at[1], got2, 2)
    share(dmsg, dgot, 1)
    down = (((1,), (1,)), ((), ()))
    for j, field in enumerate((v0, v1, v2)):
        for t in range(ny // 128):
            at = slice(t * 128, t * 128 + 128)
            tall[t] = field[2, PAD : PAD + nx, at] + field[3, PAD : PAD + nx, at]
        pairs = jnp.concatenate(
            [tall[t, pl.ds(0, nxc, 2), :] + tall[t, pl.ds(1, nxc, 2), :] for t in range(ny // 128)], axis=1
        )
        coarse = sum(lax.dot_general(part, up[...], down, preferred_element_type=F32) for part in parts_of(pairs))
        for g in range(frames):
            wq[g, j] = coarse[g * quarter : (g + 1) * quarter]
    y_sems = (y_send, y_recv)
    wg[0, f] = wq[f]
    copies_w = [send(wq.at[f], wg.at[1, f], y_sems, 0, (f, slab_at(-1)))]
    for k in range(1, frames):
        to = frame_at(k)
        copies_w.append(send(wq.at[to], wg.at[1, f], y_sems, k, (to, slab_at(-1))))
        copies_w.append(send(wq.at[to], wg.at[0, f], y_sems, frames + k, (to, s)))
    shared(got2, 2)
    place = lax.broadcasted_iota(jnp.int32, (1, 128), 1)
    c_row = jnp.zeros((1, 128), F32)
    for j, c in enumerate(cg_coefficients(moments_of(got2))):
        c_row = jnp.where(place == j, c, c_row)
    cmsg[...] = c_row
    cgot[f] = c_row
    copies_c = [send(cmsg, cgot.at[f], y_sems, 2 * frames + k, (frame_at(k), s)) for k in range(1, frames)]

    for copy in copies_w:
        copy.wait_recv()
    for copy in copies_c:
        copy.wait_recv()
    inverse = smoothing_inverse(frames)
    for side in range(2):
        w = [sum(cgot[k][:, j : j + 1] * wg[side, k, j] for j in range(3)) for k in range(frames)]
        for g in range(frames):
            uq[g, side] = sum(float(inverse[g, k]) * w[k] for k in range(frames))
    uf[f] = uq[f]
    copies_u = [send(uq.at[frame_at(k)], uf.at[f], y_sems, 3 * frames + k, (frame_at(k), s)) for k in range(1, frames)]
    shared(dgot, 1)
    misfit_ref[...] = jnp.sum(dgot[...], axis=0)
    for copy in copies_u:
        copy.wait_recv()
    u = jnp.concatenate([uf[g, 0] for g in range(frames)], axis=0)
    above = jnp.concatenate([uf[g, 1] for g in range(frames)], axis=0)
    out_ref[0] = u
    out_ref[1] = jnp.where(s < slabs - 1, above, 0.0)

    @pl.when(odd)
    def _():
        for copy in [copy_strip, copy_relay, copy_q3, relay_q3, copy_up, copy_h5b]:
            copy.wait_send()

    @pl.when(even)
    def _():
        copy_down.wait_send()
        copy_h0b.wait_send()

    for copy in [copy_cz, copy_h0, copy_h1, copy_h4, copy_h5, *copies_q, *copies_p, *copies_w, *copies_c, *copies_u]:
        copy.wait_send()


def difference(u_ref, misfit_in, out_ref, misfit_ref):
    u = u_ref[0]
    nxc, nyc = u.shape
    row_c = lax.broadcasted_iota(jnp.int32, (nxc, nyc), 0)
    lane_c = lax.broadcasted_iota(jnp.int32, (nxc, nyc), 1)
    out_ref[0] = u - u_ref[1]
    out_ref[1] = u - jnp.where(row_c < nxc - 1, pltpu.roll(u, nxc - 1, 0), 0.0)
    out_ref[2] = u - jnp.where(lane_c < nyc - 1, pltpu.roll(u, nyc - 1, 1), 0.0)
    misfit_ref[...] = misfit_in[...]


def shards(frames, slabs, labels, region_conductivity, source, receivers, observed):
    _, nx, ny = labels.shape
    nxc, nyc = nx // 2, ny // 2
    recv = receivers.shape[2]
    quarter = nxc // frames
    vmem = pl.BlockSpec(memory_space=pltpu.VMEM)
    hbm = pl.BlockSpec(memory_space=pltpu.HBM)
    plane = (PLANES, nx, ny)
    padded = (PLANES, nx + 2 * PAD, ny)
    scratch = [
        pltpu.VMEM((2, nx, ny), jnp.int32),
        pltpu.VMEM((3, nxc, nyc), F32),
        pltpu.VMEM((3, recv), jnp.int32),
        pltpu.VMEM((1, recv), F32),
        *[pltpu.VMEM(padded, F32) for _ in range(4)],
        *[pltpu.VMEM(plane, F32) for _ in range(6)],
        pltpu.VMEM((nxc, nyc), F32),
        pltpu.VMEM((4, nxc, nyc), F32),
        pltpu.VMEM((nyc, ny), BF16),
        pltpu.VMEM((ny // 128, nx, 128), F32),
        pltpu.VMEM((recv, 2 * nx), BF16),
        pltpu.VMEM((recv, ny), BF16),
        pltpu.VMEM((2, 1, 128), F32),
        pltpu.VMEM((slabs, 1, 128), F32),
        pltpu.VMEM((slabs, 1, 128), F32),
        pltpu.VMEM((3, 1, recv), F32),
        pltpu.VMEM((3, 3, 1, recv), F32),
        pltpu.VMEM((1, recv), F32),
        pltpu.VMEM((slabs, 1, recv), F32),
        pltpu.VMEM((frames, 3, quarter, nyc), F32),
        pltpu.VMEM((2, frames, 3, quarter, nyc), F32),
        pltpu.VMEM((1, 128), F32),
        pltpu.VMEM((frames, 1, 128), F32),
        pltpu.VMEM((frames, 2, quarter, nyc), F32),
        pltpu.VMEM((frames, 2, quarter, nyc), F32),
        pltpu.SemaphoreType.DMA((4,)),
        *[pltpu.SemaphoreType.DMA((5 + frames,)) for _ in range(2)],
        *[pltpu.SemaphoreType.DMA((1 + frames,)) for _ in range(2)],
        *[pltpu.SemaphoreType.DMA((5,)) for _ in range(2)],
        *[pltpu.SemaphoreType.DMA((3,)) for _ in range(2)],
        *[pltpu.SemaphoreType.DMA((3,)) for _ in range(2)],
        *[pltpu.SemaphoreType.DMA((4 * frames,)) for _ in range(2)],
        pltpu.SemaphoreType.REGULAR((2,)),
    ]
    out, misfit = pl.pallas_call(
        functools.partial(kernel, frames, slabs, region_conductivity.shape[0]),
        out_shape=(jax.ShapeDtypeStruct((2, nxc, nyc), F32), jax.ShapeDtypeStruct((1, recv), F32)),
        in_specs=[hbm, pl.BlockSpec(memory_space=pltpu.SMEM), hbm, hbm, hbm],
        out_specs=(vmem, vmem),
        scratch_shapes=scratch,
        compiler_params=pltpu.CompilerParams(
            collective_id=0, has_side_effects=True, vmem_limit_bytes=64 * 1024 * 1024
        ),
    )(labels, region_conductivity, source, jnp.transpose(receivers, (1, 0, 2)), observed)
    out, misfit = pl.pallas_call(
        difference,
        out_shape=(jax.ShapeDtypeStruct((3, nxc, nyc), F32), jax.ShapeDtypeStruct((1, recv), F32)),
        in_specs=[vmem, vmem],
        out_specs=(vmem, vmem),
    )(out, misfit)
    return out.reshape(1, 3, 1, nxc, nyc), misfit


def solution(mesh):
    in_specs = (
        P("space", None, None),
        P(),
        P("frame", None, "space", None, None),
        P("frame", None, None),
        P("frame", None),
    )
    out_specs = (P("frame", None, "space", None, None), P("frame", None))
    body = functools.partial(shards, mesh.shape["frame"], mesh.shape["space"])
    return jax.shard_map(body, mesh=mesh, in_specs=in_specs, out_specs=out_specs, check_vma=False)
```

```python
import functools

import jax
import jax.numpy as jnp
import numpy as np
from jax import lax
from jax.experimental import pallas as pl
from jax.experimental.pallas import tpu as pltpu
from jax.sharding import PartitionSpec as P

SMOOTHING = 4.0
PAD = 8
ROWS = 8
PLANES = 7
MESH = pl.DeviceIdType.MESH
F32 = jnp.float32
BF16 = jnp.bfloat16


def smoothing_inverse(frames):
    matrix = np.zeros((frames, frames))
    for f in range(frames):
        near = [g for g in (f - 1, f + 1) if 0 <= g < frames]
        matrix[f, f] = 1.0 + SMOOTHING * len(near)
        for g in near:
            matrix[f, g] = -SMOOTHING
    return np.linalg.inv(matrix)


def parts_of(x):
    high = x.astype(BF16)
    rest = x - high.astype(F32)
    middle = rest.astype(BF16)
    low = (rest - middle.astype(F32)).astype(BF16)
    return high, middle, low


def dot(a, b):
    return jnp.dot(a, b, preferred_element_type=F32)


def lanes_to_sublanes(row):
    n = row.shape[1]
    same = lax.broadcasted_iota(jnp.int32, (n, n), 0) == lax.broadcasted_iota(jnp.int32, (n, n), 1)
    return jnp.sum(jnp.where(same, row, jnp.zeros_like(row)), axis=1, keepdims=True)


def sublanes_to_lanes(column):
    n = column.shape[0]
    same = lax.broadcasted_iota(jnp.int32, (n, n), 0) == lax.broadcasted_iota(jnp.int32, (n, n), 1)
    return jnp.sum(jnp.where(same, column, jnp.zeros_like(column)), axis=0, keepdims=True)


def folded(x):
    total = x[:, :128]
    for start in range(128, x.shape[1], 128):
        total = total + x[:, start : start + 128]
    return total


def cg_coefficients(m):
    m0, m1, m2, m3, m4, m5 = m
    a0 = m0 / m1
    rr1 = m0 - 2.0 * a0 * m1 + a0 * a0 * m2
    b0 = rr1 / m0
    p0, p1 = 1.0 + b0, -a0
    a1 = rr1 / (p0 * p0 * m1 + 2.0 * p0 * p1 * m2 + p1 * p1 * m3)
    r0, r1, r2 = 1.0, -a0 - a1 * p0, -a1 * p1
    rr2 = m0 + r1 * r1 * m2 + r2 * r2 * m4 + 2.0 * (r1 * m1 + r2 * m2 + r1 * r2 * m3)
    b1 = rr2 / rr1
    q0, q1, q2 = r0 + b1 * p0, r1 + b1 * p1, r2
    curv = q0 * q0 * m1 + q1 * q1 * m3 + q2 * q2 * m5
    curv = curv + 2.0 * (q0 * q1 * m2 + q0 * q2 * m3 + q1 * q2 * m4)
    a2 = rr2 / curv
    return a0 + a1 * p0 + a2 * q0, a1 * p1 + a2 * q1, a2 * q2


def kernel(
    frames, slabs, regions,
    labels_ref, cond_ref, source_ref, recv_hbm, obs_hbm,
    out_ref, misfit_ref,
    lab, src, recv_ref, obs_ref, h, v0, v1, v2, diag, kxo, kxm, kyo, kym, kz,
    czb, qs, up, tall, gat, hot_y, msg, got1, got2, pmsg, pgot, dmsg, dgot, wq, wg, cmsg, cgot, uq, uf,
    load_sem, h_send, h_recv, g_send, g_recv, q_send, q_recv, ar_send, ar_recv, p_send, p_recv, y_send, y_recv, known,
):
    nx, ny = lab.shape[1], lab.shape[2]
    nxc, nyc = nx // 2, ny // 2
    recv = recv_ref.shape[1]
    quarter = nxc // frames
    chunks = nx // ROWS
    f = lax.axis_index("frame")
    s = lax.axis_index("space")

    def slab_at(by):
        return lax.rem(s + by + slabs, slabs)

    def frame_at(by):
        return lax.rem(f + by, frames)

    barrier = pltpu.get_barrier_semaphore()

    def tell(semaphore, slabs_by, others):
        for by in slabs_by:
            pl.semaphore_signal(semaphore, inc=1, device_id=(f, slab_at(by)), device_id_type=MESH)
        if others:
            for k in range(1, frames):
                pl.semaphore_signal(semaphore, inc=1, device_id=(frame_at(k), s), device_id_type=MESH)
        return len(slabs_by) + (frames - 1 if others else 0)

    reach = slabs // 16
    quarters = [slabs // 4, slabs // 2, slabs - slabs // 4]
    near = [by for k in range(1, reach + 1) for by in (k, -k)]
    greeted = tell(barrier, near + quarters, True)

    load_labels = pltpu.make_async_copy(labels_ref, lab, load_sem.at[0])
    load_source = pltpu.make_async_copy(source_ref.at[0, :, 0], src, load_sem.at[1])
    load_labels.start()
    load_source.start()
    load_recv = pltpu.make_async_copy(recv_hbm.at[:, 0], recv_ref, load_sem.at[2])
    load_obs = pltpu.make_async_copy(obs_hbm, obs_ref, load_sem.at[3])
    load_recv.start()
    load_obs.start()

    load_labels.wait()

    def convert(i, carry):
        p, r = i // chunks, i % chunks
        here = lab[p, pl.ds(pl.multiple_of(r * ROWS, ROWS), ROWS), :]
        value = jnp.full((ROWS, ny), 0.5 * cond_ref[0], F32)
        for region in range(1, regions):
            value = jnp.where(here == region, 0.5 * cond_ref[region], value)
        h[p + 2, pl.ds(pl.multiple_of(PAD + r * ROWS, ROWS), ROWS), :] = value
        return carry

    lax.fori_loop(0, 2 * chunks, convert, 0, unroll=chunks)
    load_source.wait()

    pl.semaphore_wait(barrier, greeted)
    heard = tell(known.at[0], [reach, -reach], True)

    def remote(src_ref, dst_ref, sems, index, device):
        return pltpu.make_async_remote_copy(
            src_ref=src_ref, dst_ref=dst_ref, send_sem=sems[0].at[index], recv_sem=sems[1].at[index],
            device_id=device, device_id_type=MESH,
        )

    def send(*args):
        copy = remote(*args)
        copy.start()
        return copy

    def plane(p):
        return h.at[p, pl.ds(PAD, nx), :]

    def strip(p):
        rows = nx // frames
        return h.at[p, pl.ds(pl.multiple_of(PAD + f * rows, ROWS), rows), :]

    def half(p, which):
        return h.at[p, pl.ds(PAD + which * (nx // 2), nx // 2), :]

    def thin(p):
        rows = nx // 2 // frames
        return h.at[p, pl.ds(pl.multiple_of(PAD + nx // 2 + f * rows, ROWS), rows), :]

    copy_cz = send(src.at[0], czb, (q_send, q_recv), 0, (f, slab_at(1)))
    h_sems = (h_send, h_recv)
    odd = lax.rem(s, 2) == 1
    copy_strip = remote(strip(2), strip(6), h_sems, 4, (f, slab_at(-2)))
    copies_strip = [remote(strip(6), strip(6), h_sems, 5 + k, (frame_at(k), s)) for k in range(1, frames)]
    copy_relay = remote(plane(4), plane(6), h_sems, 5, (f, slab_at(-1)))
    even = jnp.logical_not(odd)
    g_sems = (g_send, g_recv)
    copy_h0b = remote(half(2, 1), half(0, 1), g_sems, 0, (f, slab_at(1)))
    copy_h5b = remote(half(3, 1), half(5, 1), g_sems, 0, (f, slab_at(-1)))
    copy_up = remote(thin(2), thin(0), g_sems, 1, (f, slab_at(1)))
    copy_down = remote(thin(3), thin(5), g_sems, 1, (f, slab_at(-1)))
    copies_up = [remote(thin(0), thin(0), g_sems, 1 + k, (frame_at(k), s)) for k in range(1, frames)]
    copies_down = [remote(thin(5), thin(5), g_sems, 1 + k, (frame_at(k), s)) for k in range(1, frames)]

    @pl.when(odd)
    def _():
        copy_up.start()
        copy_strip.start()

    pl.when(even)(copy_down.start)
    copy_h1 = send(plane(3), plane(1), h_sems, 0, (f, slab_at(1)))
    copy_h4 = send(plane(2), plane(4), h_sems, 1, (f, slab_at(-1)))

    row_c = lax.broadcasted_iota(jnp.int32, (nxc, nyc), 0)
    lane_c = lax.broadcasted_iota(jnp.int32, (nxc, nyc), 1)
    along_x, along_y = src[1], src[2]
    total = src[0] + along_x - jnp.where(row_c > 0, pltpu.roll(along_x, 1, 0), 0.0)
    total = total + along_y - jnp.where(lane_c > 0, pltpu.roll(along_y, 1, 1), 0.0)
    copy_cz.wait_recv()
    qs[1] = total - jnp.where(s > 0, czb[...], 0.0)
    q_sems = (q_send, q_recv)
    copies_q = [
        send(qs.at[1], qs.at[0], q_sems, 1, (f, slab_at(1))),
        send(qs.at[1], qs.at[2], q_sems, 2, (f, slab_at(-1))),
    ]
    copy_q3 = remote(qs.at[1], qs.at[3], q_sems, 3, (f, slab_at(-2)))
    relay_q3 = remote(qs.at[2], qs.at[3], q_sems, 4, (f, slab_at(-1)))
    pl.when(odd)(copy_q3.start)

    copy_h0 = send(half(2, 0), half(0, 0), h_sems, 2, (f, slab_at(1)))
    copy_h5 = send(half(3, 0), half(5, 0), h_sems, 3, (f, slab_at(-1)))
    pl.when(even)(copy_h0b.start)
    pl.when(odd)(copy_h5b.start)
    zero_rows = jnp.zeros((PAD, ny), F32)
    for field in (h, v0, v1, v2):
        for p in range(PLANES):
            field[p, 0:PAD, :] = zero_rows
            field[p, PAD + nx : PAD + nx + PAD, :] = zero_rows
    load_recv.wait()
    load_obs.wait()
    first = 2 * s - 2
    zx_row = (recv_ref[0:1, :] - first) * nx + recv_ref[1:2, :]
    zx_col = lanes_to_sublanes(zx_row)
    y_col = lanes_to_sublanes(recv_ref[2:3, :])
    own_ids = lax.broadcasted_iota(jnp.int32, (recv, 2 * nx), 1) + 2 * nx
    gat[...] = (zx_col == own_ids).astype(BF16)
    hot_y[...] = (y_col == lax.broadcasted_iota(jnp.int32, (recv, ny), 1)).astype(BF16)
    coarse_id = lax.broadcasted_iota(jnp.int32, (nyc, ny), 0)
    up[...] = (coarse_id == lax.broadcasted_iota(jnp.int32, (nyc, ny), 1) // 2).astype(BF16)
    z_in = recv_ref[0:1, :] - 2 * s
    inside = (z_in >= 0) & (z_in < 2)

    def valid(p):
        z = first + p
        return (z >= 0) & (z < 2 * slabs)

    def aligned(r):
        return pl.ds(pl.multiple_of(PAD + r * ROWS, ROWS), ROWS)

    def next_row(field, p, r, here):
        return pltpu.roll(jnp.where(sub == 0, field[p, aligned(r + 1), :], here), ROWS - 1, 0)

    def previous_row(field, p, r, here):
        return pltpu.roll(jnp.where(sub == ROWS - 1, field[p, aligned(r - 1), :], here), 1, 0)

    def prolong(c):
        z = s - 1 + c
        ok = (z >= 0) & (z < slabs)
        high, middle, low = parts_of(jnp.where(ok, qs[c], 0.0))
        fine = dot(high, up[...]) + dot(middle, up[...]) + dot(low, up[...])
        for t in range(ny // 128):
            tall[t, pl.ds(0, nxc, 2), :] = fine[:, t * 128 : t * 128 + 128]
            tall[t, pl.ds(1, nxc, 2), :] = fine[:, t * 128 : t * 128 + 128]
        for p in (2 * c, 2 * c + 1):
            if p < PLANES:
                for t in range(ny // 128):
                    v0[p, PAD : PAD + nx, t * 128 : t * 128 + 128] = tall[t]

    lane = lax.broadcasted_iota(jnp.int32, (ROWS, ny), 1)
    sub = lax.broadcasted_iota(jnp.int32, (ROWS, ny), 0)

    def zero_outside(p):
        @pl.when(jnp.logical_not(valid(p)))
        def _():
            h[p, PAD : PAD + nx, :] = jnp.zeros((nx, ny), F32)

    def vertical(e):
        keep = jnp.where(valid(e) & valid(e + 1), 1.0, 0.0).astype(F32)

        def body(r, carry):
            kz[e, pl.ds(pl.multiple_of(r * ROWS, ROWS), ROWS), :] = keep * (h[e, aligned(r), :] + h[e + 1, aligned(r), :])
            return carry

        lax.fori_loop(0, chunks, body, 0, unroll=chunks)

    def coefficients(p):
        def body(r, carry):
            at = pl.ds(pl.multiple_of(r * ROWS, ROWS), ROWS)
            here = h[p, aligned(r), :]
            x_next, x_prev = next_row(h, p, r, here), previous_row(h, p, r, here)
            y_next = jnp.where(lane < ny - 1, pltpu.roll(here, ny - 1, 1), 0.0)
            y_prev = jnp.where(lane > 0, pltpu.roll(here, 1, 1), 0.0)
            kxo[p, at, :] = here + x_next
            kxm[p, at, :] = here + x_prev
            kyo[p, at, :] = jnp.where(lane < ny - 1, here + y_next, 0.0)
            kym[p, at, :] = jnp.where(lane > 0, here + y_prev, 0.0)
            near = x_next + x_prev + y_next + y_prev
            diag[p, at, :] = 6.0 * here + near + h[p - 1, aligned(r), :] + h[p + 1, aligned(r), :]
            return carry

        lax.fori_loop(0, chunks, body, 0, unroll=chunks)

    def operate(src_v, dst_v, p, with_moments, sums):
        def body(r, carry):
            at = pl.ds(pl.multiple_of(r * ROWS, ROWS), ROWS)
            here = src_v[p, aligned(r), :]
            value = diag[p, at, :] * here
            value = value - kxo[p, at, :] * next_row(src_v, p, r, here)
            value = value - kxm[p, at, :] * previous_row(src_v, p, r, here)
            value = value - kyo[p, at, :] * pltpu.roll(here, ny - 1, 1)
            value = value - kym[p, at, :] * pltpu.roll(here, 1, 1)
            value = value - kz[p, at, :] * src_v[p + 1, aligned(r), :]
            value = value - kz[p - 1, at, :] * src_v[p - 1, aligned(r), :]
            dst_v[p, aligned(r), :] = value
            if not with_moments:
                return carry
            return (carry[0] + folded(here * value), carry[1] + folded(value * value))

        return lax.fori_loop(0, chunks, body, sums, unroll=chunks)

    def square(src_v, p, total):
        def body(r, carry):
            here = src_v[p, aligned(r), :]
            return carry + folded(here * here)

        return lax.fori_loop(0, chunks, body, total, unroll=chunks)

    def energy(field, p, total):
        def body(r, carry):
            at = pl.ds(pl.multiple_of(r * ROWS, ROWS), ROWS)
            here = field[p, aligned(r), :]
            near = kxo[p, at, :] * next_row(field, p, r, here)
            near = near + kyo[p, at, :] * pltpu.roll(here, ny - 1, 1)
            near = near + kz[p, at, :] * field[p + 1, aligned(r), :]
            return carry + folded(here * (diag[p, at, :] * here - 2.0 * near))

        return lax.fori_loop(0, chunks, body, total, unroll=chunks)

    nothing = jnp.zeros((ROWS, 128), F32)

    def krylov_own():
        m0 = square(v0, 3, square(v0, 2, nothing))
        return m0, operate(v0, v1, 3, True, operate(v0, v1, 2, True, (nothing, nothing)))

    def krylov_near():
        for p in (1, 4):
            operate(v0, v1, p, False, 0)
        m34 = operate(v1, v2, 3, True, operate(v1, v2, 2, True, (nothing, nothing)))
        return m34, energy(v2, 2, nothing)

    def krylov_far(m5):
        operate(v0, v1, 5, False, 0)
        operate(v1, v2, 4, False, 0)
        return energy(v2, 3, m5)

    def summed(*moments):
        place = lax.broadcasted_iota(jnp.int32, (1, 128), 1)
        row = jnp.zeros((1, 128), F32)
        for j, m in enumerate(moments):
            row = jnp.where(place == j, jnp.sum(jnp.sum(m, axis=0, keepdims=True), axis=1, keepdims=True), row)
        return row

    def share(source, landing, index):
        def start(i, carry):
            k = lax.rem(i + slabs // 2, slabs - 1) + 1
            pltpu.make_async_remote_copy(
                src_ref=source, dst_ref=landing.at[s], send_sem=ar_send.at[index], recv_sem=ar_recv.at[index],
                device_id=(f, slab_at(k)), device_id_type=MESH,
            ).start()
            return carry

        lax.fori_loop(0, slabs - 1, start, 0)

    def shared(landing, index):
        others = landing.at[pl.ds(0, slabs - 1)]
        whole = pltpu.make_async_remote_copy(
            src_ref=others, dst_ref=others, send_sem=ar_send.at[index], recv_sem=ar_recv.at[index],
            device_id=(f, slab_at(1)), device_id_type=MESH,
        )
        whole.wait_recv()
        return whole

    def moments_of(landing):
        total = jnp.sum(landing[...], axis=0)
        return [total[:, j : j + 1] for j in range(6)]

    @pl.when(odd)
    def _():
        copy_down.wait_recv()
        for copy in copies_down:
            copy.start()
        copy_strip.wait_recv()
        for copy in copies_strip:
            copy.start()

    @pl.when(even)
    def _():
        copy_up.wait_recv()
        for copy in copies_up:
            copy.start()

    copy_h1.wait_recv()
    copy_h4.wait_recv()
    zero_outside(1)
    zero_outside(4)
    pl.when(odd)(copy_relay.start)
    for e in (1, 2, 3):
        vertical(e)
    for p in (2, 3):
        coefficients(p)
    pl.semaphore_wait(known.at[0], heard)
    heard = tell(known.at[1], quarters, False)
    for copy in copies_q:
        copy.wait_recv()
    pl.when(odd)(relay_q3.start)
    for c in range(3):
        prolong(c)
    m0, m12 = krylov_own()
    copy_h0.wait_recv()
    copy_h5.wait_recv()

    @pl.when(odd)
    def _():
        copy_h0b.wait_recv()
        for copy in copies_down:
            copy.wait()

    @pl.when(even)
    def _():
        copy_h5b.wait_recv()
        for copy in copies_up:
            copy.wait()

    zero_outside(0)
    zero_outside(5)
    vertical(0)
    vertical(4)
    coefficients(1)
    coefficients(4)
    m34, m5 = krylov_near()

    @pl.when(odd)
    def _():
        copy_q3.wait_recv()
        for copy in copies_strip:
            copy.wait()

    @pl.when(jnp.logical_not(odd))
    def _():
        relay_q3.wait_recv()
        copy_relay.wait_recv()

    prolong(3)
    zero_outside(6)
    vertical(5)
    coefficients(5)
    m5 = krylov_far(m5)
    moments = summed(m0, *m12, *m34, m5)
    msg[0] = moments
    got1[s] = moments
    pl.semaphore_wait(known.at[1], heard)
    share(msg.at[0], got1, 0)

    for j, field in enumerate((v0, v1, v2)):
        whole = jnp.concatenate([field[2, PAD : PAD + nx, :], field[3, PAD : PAD + nx, :]], axis=0)
        rows = sum(dot(gat[...], part) for part in parts_of(whole))
        column = jnp.sum(rows * hot_y[...].astype(F32), axis=1, keepdims=True)
        pmsg[j] = sublanes_to_lanes(column)
    p_sems = (p_send, p_recv)
    copies_p = [
        send(pmsg, pgot.at[0], p_sems, 0, (f, slab_at(1))),
        send(pmsg, pgot.at[1], p_sems, 1, (f, slab_at(-1))),
        send(pmsg, pgot.at[2], p_sems, 2, (f, slab_at(-2))),
    ]
    sent1 = shared(got1, 0)
    c0, c1, c2 = cg_coefficients(moments_of(got1))
    observed = obs_ref[...]

    def misfit(values):
        return c0 * values[0] + c1 * values[1] + c2 * values[2] - observed

    mine = jnp.where(inside, misfit([pmsg[j] for j in range(3)]), 0.0)
    dmsg[...] = mine
    dgot[s] = mine
    for copy in copies_p:
        copy.wait_recv()
    d = misfit([pmsg[j] + pgot[0, j] + pgot[1, j] + pgot[2, j] for j in range(3)])

    d_parts = parts_of(d)
    for p in range(PLANES):
        hit = zx_row == lax.broadcasted_iota(jnp.int32, (nx, recv), 0) + p * nx
        value = sum(dot(jnp.where(hit, part.astype(F32), 0.0).astype(BF16), hot_y[...]) for part in d_parts)
        v0[p, PAD : PAD + nx, :] = jnp.where(valid(p), value, 0.0)
    m0, m12 = krylov_own()
    m34, m5 = krylov_near()
    moments = summed(m0, *m12, *m34, krylov_far(m5))
    msg[1] = moments
    got2[s] = moments
    share(msg.at[1], got2, 2)
    down = (((1,), (1,)), ((), ()))
    for j, field in enumerate((v0, v1, v2)):
        for t in range(ny // 128):
            at = slice(t * 128, t * 128 + 128)
            tall[t] = field[2, PAD : PAD + nx, at] + field[3, PAD : PAD + nx, at]
        pairs = jnp.concatenate(
            [tall[t, pl.ds(0, nxc, 2), :] + tall[t, pl.ds(1, nxc, 2), :] for t in range(ny // 128)], axis=1
        )
        coarse = sum(lax.dot_general(part, up[...], down, preferred_element_type=F32) for part in parts_of(pairs))
        for g in range(frames):
            wq[g, j] = coarse[g * quarter : (g + 1) * quarter]
    y_sems = (y_send, y_recv)
    wg[0, f] = wq[f]
    copies_w = [send(wq.at[f], wg.at[1, f], y_sems, 0, (f, slab_at(-1)))]
    for k in range(1, frames):
        to = frame_at(k)
        copies_w.append(send(wq.at[to], wg.at[1, f], y_sems, k, (to, slab_at(-1))))
        copies_w.append(send(wq.at[to], wg.at[0, f], y_sems, frames + k, (to, s)))
    share(dmsg, dgot, 1)
    sent2 = shared(got2, 2)
    place = lax.broadcasted_iota(jnp.int32, (1, 128), 1)
    c_row = jnp.zeros((1, 128), F32)
    for j, c in enumerate(cg_coefficients(moments_of(got2))):
        c_row = jnp.where(place == j, c, c_row)
    cmsg[...] = c_row
    cgot[f] = c_row
    copies_c = [send(cmsg, cgot.at[f], y_sems, 2 * frames + k, (frame_at(k), s)) for k in range(1, frames)]

    for copy in copies_w:
        copy.wait_recv()
    for copy in copies_c:
        copy.wait_recv()
    inverse = smoothing_inverse(frames)
    for side in range(2):
        w = [sum(cgot[k][:, j : j + 1] * wg[side, k, j] for j in range(3)) for k in range(frames)]
        for g in range(frames):
            uq[g, side] = sum(float(inverse[g, k]) * w[k] for k in range(frames))
    uf[f] = uq[f]
    copies_u = [send(uq.at[frame_at(k)], uf.at[f], y_sems, 3 * frames + k, (frame_at(k), s)) for k in range(1, frames)]
    sent3 = shared(dgot, 1)
    misfit_ref[...] = jnp.sum(dgot[...], axis=0)
    for copy in copies_u:
        copy.wait_recv()
    u = jnp.concatenate([uf[g, 0] for g in range(frames)], axis=0)
    above = jnp.concatenate([uf[g, 1] for g in range(frames)], axis=0)
    out_ref[0] = u
    out_ref[1] = jnp.where(s < slabs - 1, above, 0.0)

    @pl.when(odd)
    def _():
        for copy in [copy_strip, copy_relay, copy_q3, relay_q3, copy_up, copy_h5b]:
            copy.wait_send()

    @pl.when(even)
    def _():
        copy_down.wait_send()
        copy_h0b.wait_send()

    for copy in [copy_cz, copy_h0, copy_h1, copy_h4, copy_h5, *copies_q, *copies_p, *copies_w, *copies_c, *copies_u, sent1, sent2, sent3]:
        copy.wait_send()


def difference(u_ref, misfit_in, out_ref, misfit_ref):
    u = u_ref[0]
    nxc, nyc = u.shape
    row_c = lax.broadcasted_iota(jnp.int32, (nxc, nyc), 0)
    lane_c = lax.broadcasted_iota(jnp.int32, (nxc, nyc), 1)
    out_ref[0] = u - u_ref[1]
    out_ref[1] = u - jnp.where(row_c < nxc - 1, pltpu.roll(u, nxc - 1, 0), 0.0)
    out_ref[2] = u - jnp.where(lane_c < nyc - 1, pltpu.roll(u, nyc - 1, 1), 0.0)
    misfit_ref[...] = misfit_in[...]


def shards(frames, slabs, labels, region_conductivity, source, receivers, observed):
    _, nx, ny = labels.shape
    nxc, nyc = nx // 2, ny // 2
    recv = receivers.shape[2]
    quarter = nxc // frames
    vmem = pl.BlockSpec(memory_space=pltpu.VMEM)
    hbm = pl.BlockSpec(memory_space=pltpu.HBM)
    plane = (PLANES, nx, ny)
    padded = (PLANES, nx + 2 * PAD, ny)
    scratch = [
        pltpu.VMEM((2, nx, ny), jnp.int32),
        pltpu.VMEM((3, nxc, nyc), F32),
        pltpu.VMEM((3, recv), jnp.int32),
        pltpu.VMEM((1, recv), F32),
        *[pltpu.VMEM(padded, F32) for _ in range(4)],
        *[pltpu.VMEM(plane, F32) for _ in range(6)],
        pltpu.VMEM((nxc, nyc), F32),
        pltpu.VMEM((4, nxc, nyc), F32),
        pltpu.VMEM((nyc, ny), BF16),
        pltpu.VMEM((ny // 128, nx, 128), F32),
        pltpu.VMEM((recv, 2 * nx), BF16),
        pltpu.VMEM((recv, ny), BF16),
        pltpu.VMEM((2, 1, 128), F32),
        pltpu.VMEM((slabs, 1, 128), F32),
        pltpu.VMEM((slabs, 1, 128), F32),
        pltpu.VMEM((3, 1, recv), F32),
        pltpu.VMEM((3, 3, 1, recv), F32),
        pltpu.VMEM((1, recv), F32),
        pltpu.VMEM((slabs, 1, recv), F32),
        pltpu.VMEM((frames, 3, quarter, nyc), F32),
        pltpu.VMEM((2, frames, 3, quarter, nyc), F32),
        pltpu.VMEM((1, 128), F32),
        pltpu.VMEM((frames, 1, 128), F32),
        pltpu.VMEM((frames, 2, quarter, nyc), F32),
        pltpu.VMEM((frames, 2, quarter, nyc), F32),
        pltpu.SemaphoreType.DMA((4,)),
        *[pltpu.SemaphoreType.DMA((5 + frames,)) for _ in range(2)],
        *[pltpu.SemaphoreType.DMA((1 + frames,)) for _ in range(2)],
        *[pltpu.SemaphoreType.DMA((5,)) for _ in range(2)],
        *[pltpu.SemaphoreType.DMA((3,)) for _ in range(2)],
        *[pltpu.SemaphoreType.DMA((3,)) for _ in range(2)],
        *[pltpu.SemaphoreType.DMA((4 * frames,)) for _ in range(2)],
        pltpu.SemaphoreType.REGULAR((2,)),
    ]
    out, misfit = pl.pallas_call(
        functools.partial(kernel, frames, slabs, region_conductivity.shape[0]),
        out_shape=(jax.ShapeDtypeStruct((2, nxc, nyc), F32), jax.ShapeDtypeStruct((1, recv), F32)),
        in_specs=[hbm, pl.BlockSpec(memory_space=pltpu.SMEM), hbm, hbm, hbm],
        out_specs=(vmem, vmem),
        scratch_shapes=scratch,
        compiler_params=pltpu.CompilerParams(
            collective_id=0, has_side_effects=True, vmem_limit_bytes=64 * 1024 * 1024
        ),
    )(labels, region_conductivity, source, jnp.transpose(receivers, (1, 0, 2)), observed)
    out, misfit = pl.pallas_call(
        difference,
        out_shape=(jax.ShapeDtypeStruct((3, nxc, nyc), F32), jax.ShapeDtypeStruct((1, recv), F32)),
        in_specs=[vmem, vmem],
        out_specs=(vmem, vmem),
    )(out, misfit)
    return out.reshape(1, 3, 1, nxc, nyc), misfit


def solution(mesh):
    in_specs = (
        P("space", None, None),
        P(),
        P("frame", None, "space", None, None),
        P("frame", None, None),
        P("frame", None),
    )
    out_specs = (P("frame", None, "space", None, None), P("frame", None))
    body = functools.partial(shards, mesh.shape["frame"], mesh.shape["space"])
    return jax.shard_map(body, mesh=mesh, in_specs=in_specs, out_specs=out_specs, check_vma=False)
```
